256 devices in a mesh: feat: 16 (over y, x), rep: 16 (over z, core).
Axes of the slice: x: 4, y: 4, z: 8, core: 2. Of those that a mesh axis runs over, the one named last changes fastest.
Arguments:
- feature_table: bfloat16 [768, 32768], P('feat'), may hold values from -6 to 6
- node_ids: int32 [16, 8192], P('rep'), may hold values from 0 to 32767
- neigh_one: int32 [16, 15, 2048], P('rep'), may hold values from 0 to 511
- count_one: int32 [16, 2048], P('rep'), may hold values from 1 to 15
- neigh_two: int32 [16, 25, 1024], P('rep', None, 'feat'), may hold values from 0 to 127
- count_two: int32 [16, 1024], P('rep', 'feat'), may hold values from 1 to 25
- w_one_self: bfloat16 [768, 1024], P('feat'), may hold values from -0.21875 to 0.21875
- w_one_neigh: bfloat16 [768, 1024], P('feat'), may hold values from -0.21875 to 0.21875
- w_two_self: bfloat16 [1024, 153], replicated, may hold values from -0.1875 to 0.1875
- w_two_neigh: bfloat16 [1024, 153], replicated, may hold values from -0.1875 to 0.1875
- logit_grad: bfloat16 [16, 1024, 153], P('rep', 'feat'), may hold values from -0.046875 to 0.046875
Outputs:
- logits: bfloat16 [16, 1024, 153], P('rep', 'feat')
- grad_w1_self: float32 [768, 1024], P('feat')
- grad_w1_neigh: float32 [768, 1024], P('feat')
- grad_w2_self: float32 [1024, 153], replicated
- grad_w2_neigh: float32 [1024, 153], replicated
The draws below stay inside these ranges and needn't reach their ends.
Inputs may be any that keep to these rules, and one draw needn't show every extreme that they name: `count_one`: slots at or beyond a node's count are padding and ignored; a count reaches its fanout on some rows.
All inputs are finite; a program needn't handle non-finite values.
Results may differ from the reference program's by a relative error of at most 0.0051.
Values may be sent and summed in bfloat16 or wider, within the bound.
No kernel may reach another device: no remote copies, remote signals or barrier semaphores. Data moves between devices by JAX's collectives and lax.ppermute only.
A program may use at most 64 MiB of HBM per device.

```python
import jax
import jax.numpy as jnp
from jax import lax

D_IN = 768
HID = 1024
CLASSES = 153
FAN1 = 15
FAN2 = 25
N1_DEV = 128
TABLE = 32768
N0_DEV = 512
B_DEV = 64
N_FEAT = 16
N_REP = 16


def set_ends(array, key, least, top_value):
    longest = array.shape.index(max(array.shape))
    spots = []
    for shift in (0, 1):
        where = [jax.random.randint(jax.random.fold_in(key, axis), (), 0, length) for axis, length in enumerate(array.shape)]
        where[longest] = (where[longest] + shift) % array.shape[longest]
        spots.append(tuple(where))
    return array.at[spots[0]].set(least).at[spots[1]].set(top_value)


def steps_of(stream_key, dims, split, least, largest):
    level, own = 1.0, jax.random.fold_in(stream_key, 6)
    for axis_at, parts in split:
        heights = jnp.exp(jax.random.uniform(jax.random.fold_in(own, axis_at), (parts,), jnp.float32, least / len(split), largest / len(split)))
        level = level * jnp.repeat(heights, dims[axis_at] // parts).reshape([-1 if axis == axis_at else 1 for axis in range(len(dims))])
    return level


def centred(key, shape, deviation, bound, shards=(), kind=jnp.bfloat16):
    drawn = jax.random.normal(key, shape, jnp.float32) * deviation
    if len(shards) > 0:
        drawn = steps_of(key, shape, shards, -0.22, 0.18) * drawn
    return jnp.clip(drawn, min=-bound, max=bound).astype(kind)


def setup_inputs(seed: int = 0) -> dict:
    splits = jax.random.split(jax.random.key(seed), 12)
    feature_table = centred(splits[0], (D_IN, TABLE), 1.0, 6.0, ((0, 16),))
    node_ids = set_ends(jax.random.randint(splits[1], (N_REP, N_FEAT * N0_DEV), 0, TABLE), jax.random.fold_in(splits[1], 1), 0, TABLE - 1).astype(jnp.int32)
    neigh_one = set_ends(jax.random.randint(splits[2], (N_REP, FAN1, N_FEAT * N1_DEV), 0, N0_DEV), jax.random.fold_in(splits[2], 1), 0, N0_DEV - 1).astype(jnp.int32)
    count_one = set_ends(jax.random.randint(splits[3], (N_REP, N_FEAT * N1_DEV), 1, FAN1 + 1), jax.random.fold_in(splits[3], 1), 1, FAN1).astype(jnp.int32)
    neigh_two = set_ends(jax.random.randint(splits[4], (N_REP, FAN2, N_FEAT * B_DEV), 0, N1_DEV), jax.random.fold_in(splits[4], 1), 0, N1_DEV - 1).astype(jnp.int32)
    count_two = set_ends(jax.random.randint(splits[5], (N_REP, N_FEAT * B_DEV), 1, FAN2 + 1), jax.random.fold_in(splits[5], 1), 1, FAN2).astype(jnp.int32)
    w_one_self = centred(splits[6], (D_IN, HID), D_IN ** -0.5, 0.21875, ((0, 16),))
    w_one_neigh = centred(splits[7], (D_IN, HID), D_IN ** -0.5, 0.21875, ((0, 16),))
    w_two_self = centred(splits[8], (HID, CLASSES), HID ** -0.5, 0.1875)
    w_two_neigh = centred(splits[9], (HID, CLASSES), HID ** -0.5, 0.1875)
    logit_grad = centred(splits[10], (N_REP, N_FEAT * B_DEV, CLASSES), (1.0 / (N_REP * N_FEAT * B_DEV) ** 0.5), 0.046875, ((0, 16), (1, 16)))
    return {"feature_table": feature_table, "node_ids": node_ids, "neigh_one": neigh_one, "count_one": count_one, "neigh_two": neigh_two, "count_two": count_two, "w_one_self": w_one_self, "w_one_neigh": w_one_neigh, "w_two_self": w_two_self, "w_two_neigh": w_two_neigh, "logit_grad": logit_grad}


def gelu_tanh(values):
    return jax.nn.gelu(values, approximate=True)

def mean_rows(source, lookup, counts):
    picked = jnp.take(source, lookup, axis=0).astype(jnp.float32)
    slot_ids = lax.broadcasted_iota(jnp.int32, lookup.shape, 1)
    live_slots = (slot_ids < counts[:, None])[:, :, None]
    summed = lax.optimization_barrier(jnp.sum(jnp.where(live_slots, picked, 0.0), axis=1))
    return summed / counts.astype(jnp.float32)[:, None]

def contract_rows(first_op, second_op):
    return lax.dot_general(first_op, second_op, (((0,), (0,)), ((), ())), preferred_element_type=jnp.float32)

def contract_cols(first_op, second_op):
    return lax.dot_general(first_op, second_op, (((1,), (1,)), ((), ())), preferred_element_type=jnp.float32)

def reference(feature_table, node_ids, neigh_one, count_one, neigh_two, count_two, w_one_self, w_one_neigh, w_two_self, w_two_neigh, logit_grad):

    def replica(accum, replica_data):
        ids_here, nb_one_t, cnt_one, nb_two_t, cnt_two, upstream = replica_data
        nb_one = nb_one_t.T
        nb_two = nb_two_t.T
        inputs = jnp.take(feature_table, ids_here, axis=1).T
        offsets = jnp.arange(N_FEAT * N1_DEV, dtype=jnp.int32) // N1_DEV * N0_DEV
        self_one = inputs.reshape(N_FEAT, N0_DEV, D_IN)[:, :N1_DEV].reshape(N_FEAT * N1_DEV, D_IN)
        agg_one = mean_rows(inputs, nb_one + offsets[:, None], cnt_one).astype(jnp.bfloat16)
        pre_one = jnp.dot(self_one, w_one_self, preferred_element_type=jnp.float32) + jnp.dot(agg_one, w_one_neigh, preferred_element_type=jnp.float32)
        hidden_one = gelu_tanh(pre_one).astype(jnp.bfloat16)
        self_two = hidden_one.reshape(N_FEAT, N1_DEV, HID)[:, :B_DEV].reshape(N_FEAT * B_DEV, HID)
        target_pos = jnp.arange(N_FEAT * B_DEV, dtype=jnp.int32)
        offsets_two = target_pos // B_DEV * N1_DEV
        index_two = nb_two + offsets_two[:, None]
        agg_two = mean_rows(hidden_one, index_two, cnt_two).astype(jnp.bfloat16)
        scores = jnp.dot(self_two, w_two_self, preferred_element_type=jnp.float32) + jnp.dot(agg_two, w_two_neigh, preferred_element_type=jnp.float32)
        grad_two_self = contract_rows(self_two, upstream)
        grad_two_neigh = contract_rows(agg_two, upstream)
        grad_self_rows = contract_cols(upstream, w_two_self)
        grad_agg_rows = contract_cols(upstream, w_two_neigh) / cnt_two.astype(jnp.float32)[:, None]
        slot_ids = lax.broadcasted_iota(jnp.int32, nb_two.shape, 1)
        live_slots = (slot_ids < cnt_two[:, None]).astype(jnp.float32)
        spread_rows = (live_slots[:, :, None] * grad_agg_rows[:, None, :]).reshape(-1, HID)
        grad_hidden = jnp.zeros((N_FEAT * N1_DEV, HID), jnp.float32)
        grad_hidden = grad_hidden.at[index_two.reshape(-1)].add(spread_rows)
        grad_hidden = grad_hidden.at[offsets_two + target_pos % B_DEV].add(grad_self_rows)
        pullback = jax.vjp(gelu_tanh, pre_one)[1]
        grad_pre = pullback(grad_hidden)[0].astype(jnp.bfloat16)
        grad_one_self = contract_rows(self_one, grad_pre)
        grad_one_neigh = contract_rows(agg_one, grad_pre)
        new_accum = (accum[0] + grad_one_self, accum[1] + grad_one_neigh, accum[2] + grad_two_self, accum[3] + grad_two_neigh)
        return (new_accum, scores.astype(jnp.bfloat16))
    start_accum = (jnp.zeros((D_IN, HID), jnp.float32), jnp.zeros((D_IN, HID), jnp.float32), jnp.zeros((HID, CLASSES), jnp.float32), jnp.zeros((HID, CLASSES), jnp.float32))
    final_accum, logits = lax.scan(replica, start_accum, (node_ids, neigh_one, count_one, neigh_two, count_two, logit_grad))
    return (logits, final_accum[0], final_accum[1], final_accum[2], final_accum[3])
```

```python
import functools

import jax
import jax.numpy as jnp
import numpy as np
from jax import lax
from jax.experimental import pallas as pl
from jax.experimental.pallas import tpu as pltpu
from jax.sharding import Mesh, PartitionSpec as P

BF = jnp.bfloat16
F32 = jnp.float32
GELU_C = 0.7978845608028654
FEAT = ("y", "x")
REP = ("z", "c")
SUB = 128
INP = 512
TGT = 64
CHUNK = 512
CLS_ROWS = 10


def mm(first, second):
    return jnp.dot(first, second, preferred_element_type=F32)


def mm_nt(first, second):
    return lax.dot_general(first, second, (((1,), (1,)), ((), ())), preferred_element_type=F32)


def vmem(count):
    return [pl.BlockSpec(memory_space=pltpu.VMEM)] * count


def gather_kernel(ids_ref, neigh_ref, count_ref, table_ref, out_ref, turned, rows):
    cols, papers = table_ref.shape

    def turn(step, carry):
        start = pl.multiple_of(step * CHUNK, CHUNK)
        block = table_ref[:, pl.ds(start, CHUNK)].astype(F32)
        turned[pl.ds(start, CHUNK), :cols] = block.T
        return carry

    lax.fori_loop(0, papers // CHUNK, turn, 0, unroll=2)

    position = lax.broadcasted_iota(jnp.int32, (INP // 2, SUB), 0).astype(F32).astype(BF)
    one = jnp.ones((INP // 2, SUB), BF)
    zero = jnp.zeros((INP // 2, SUB), BF)

    def sub_batch(g, carry):
        base = g * INP
        for j in range(INP):
            rows[pl.ds(j, 1), :] = turned[pl.ds(ids_ref[0, base + j], 1), :]
        nodes = pl.ds(pl.multiple_of(g * SUB, SUB), SUB)
        count = count_ref[:, nodes]
        halves = [zero, zero]
        for k in range(neigh_ref.shape[1]):
            near = jnp.where(k < count, neigh_ref[0, pl.ds(k, 1), nodes], -1)
            for h in range(2):
                here = (near - h * (INP // 2)).astype(F32).astype(BF)
                halves[h] = halves[h] + jnp.where(position == here, one, zero)
        picked = rows[...].T[:cols].astype(BF)
        summed = mm(picked[:, : INP // 2], halves[0]) + mm(picked[:, INP // 2 :], halves[1])
        agg = (summed / count.astype(F32)).astype(BF)
        own = picked[:, :SUB]
        lanes = pl.ds(pl.multiple_of((g % 4) * SUB, SUB), SUB)
        for x in range(4):
            out_ref[(g // 4) * 4 + x, :cols, lanes] = own
            out_ref[(g // 4) * 4 + x, cols:, lanes] = agg
        return carry

    lax.fori_loop(0, 16, sub_batch, 0)


def gather(node_ids, neigh_one, count_one, feature_table):
    cols, papers = feature_table.shape
    return pl.pallas_call(
        gather_kernel,
        out_shape=jax.ShapeDtypeStruct((16, 2 * cols, 4 * SUB), BF),
        in_specs=[pl.BlockSpec(memory_space=pltpu.SMEM)] + vmem(3),
        out_specs=pl.BlockSpec(memory_space=pltpu.VMEM),
        scratch_shapes=[pltpu.VMEM((papers, 128), F32), pltpu.VMEM((INP, 128), F32)],
        compiler_params=pltpu.CompilerParams(vmem_limit_bytes=48 * 2**20),
        cost_estimate=pl.CostEstimate(flops=30_000_000_000, bytes_accessed=5_000_000, transcendentals=0),
        name="gather",
    )(node_ids, neigh_one, count_one, feature_table)


def prepare_kernel(w_ref, up_ref, neigh_ref, count_ref, w2s_ref, w2n_ref, wt_ref, gh_ref, spread_ref, upt_ref):
    wt_ref[...] = w_ref[...].T
    position = lax.broadcasted_iota(jnp.int32, (SUB, TGT), 0)
    for g in range(4):
        count = count_ref[pl.ds(g, 1), :]
        spread = jnp.zeros((SUB, TGT), F32)
        for k in range(25):
            near = jnp.where(k < count, neigh_ref[g, pl.ds(k, 1), :], -1)
            spread = spread + jnp.where(position == near, 1.0, 0.0)
        spread = spread.astype(BF)
        spread_ref[g] = spread
        upstream = up_ref[g]
        own = mm(upstream, w2s_ref[...])
        near_grad = mm(upstream, w2n_ref[...]).T / count.astype(F32)
        high = near_grad.astype(BF)
        low = (near_grad - high.astype(F32)).astype(BF)
        grad = mm_nt(high, spread) + mm_nt(low, spread)
        gh_ref[:, g * SUB : (g + 1) * SUB] = grad + jnp.concatenate([own.T, jnp.zeros(own.T.shape, F32)], axis=1)
        upt_ref[:153, g * TGT : (g + 1) * TGT] = upstream.astype(F32).T.astype(BF)
    upt_ref[153:] = jnp.zeros((7, 4 * TGT), BF)


def prepare(w_x, up_y, neigh_y, count_y, w2s_x, w2n_x):
    return pl.pallas_call(
        prepare_kernel,
        out_shape=(
            jax.ShapeDtypeStruct((256, 1536), BF),
            jax.ShapeDtypeStruct((256, 4 * SUB), F32),
            jax.ShapeDtypeStruct((4, SUB, TGT), BF),
            jax.ShapeDtypeStruct((160, 4 * TGT), BF),
        ),
        in_specs=vmem(6),
        out_specs=tuple(vmem(4)),
        cost_estimate=pl.CostEstimate(flops=6_000_000_000, bytes_accessed=2_000_000, transcendentals=0),
        name="prepare",
    )(w_x, up_y, neigh_y, count_y, w2s_x, w2n_x)


def layers_kernel(st_ref, wt_ref, gh_ref, spread_ref, count_ref, upt_ref, w2_ref, grads_ref, scores_ref):
    pre = mm(wt_ref[...], st_ref[...])
    square = pre * pre
    bend = jnp.tanh(GELU_C * pre * (1.0 + 0.044715 * square))
    half = 0.5 * (1.0 + bend)
    hidden = (pre * half).astype(BF)
    slope = half + 0.5 * pre * (1.0 - bend * bend) * (GELU_C * (1.0 + 3.0 * 0.044715 * square))
    grad_pre = (gh_ref[...] * slope).astype(BF)
    grad = mm_nt(st_ref[...], grad_pre).astype(BF)
    rows = grad.shape[0] // 16
    for f in range(16):
        grads_ref[f, :rows] = grad[f * rows : (f + 1) * rows]
    own, near = [], []
    for g in range(4):
        nodes = hidden[:, g * SUB : (g + 1) * SUB]
        own.append(nodes[:, :TGT])
        near.append((mm(nodes, spread_ref[g]) / count_ref[pl.ds(g, 1), :].astype(F32)).astype(BF))
    both = jnp.concatenate([jnp.concatenate(own, axis=1), jnp.concatenate(near, axis=1)], axis=0)
    scores_ref[...] = mm(w2_ref[...], both).T
    head = mm_nt(upt_ref[...], both)
    for f in range(16):
        part = head[f * CLS_ROWS : (f + 1) * CLS_ROWS].astype(BF)
        grads_ref[f, 96 : 96 + CLS_ROWS] = part[:, :256]
        grads_ref[f, 112 : 112 + CLS_ROWS] = part[:, 256:]
        grads_ref[f, 96 + CLS_ROWS : 112] = jnp.zeros((16 - CLS_ROWS, 256), BF)
        grads_ref[f, 112 + CLS_ROWS :] = jnp.zeros((16 - CLS_ROWS, 256), BF)


def layers(st, wt, gh, spread, count_y, upt, w2_x):
    return pl.pallas_call(
        layers_kernel,
        out_shape=(
            jax.ShapeDtypeStruct((16, 128, 256), BF),
            jax.ShapeDtypeStruct((4 * TGT, 153), F32),
        ),
        in_specs=vmem(7),
        out_specs=tuple(vmem(2)),
        cost_estimate=pl.CostEstimate(flops=6_000_000_000, bytes_accessed=4_000_000, transcendentals=200_000),
        name="layers",
    )(st, wt, gh, spread, count_y, upt, w2_x)


def sum_feat_kernel(in_ref, out_ref):
    for x in range(4):
        total = sum(in_ref[4 * y + x].astype(F32) for y in range(4))
        for h in range(2):
            half = total[:, h * 128 : (h + 1) * 128]
            z = 2 * x + h
            out_ref[2 * z, :48] = half[:48]
            out_ref[2 * z + 1, :48] = half[48:96]
            out_ref[z, 48:] = half[96:112]
            out_ref[8 + z, 48:] = half[112:]


def sum_feat(parts):
    return pl.pallas_call(
        sum_feat_kernel,
        out_shape=jax.ShapeDtypeStruct((16, 64, 128), F32),
        in_specs=vmem(1),
        out_specs=vmem(1)[0],
        cost_estimate=pl.CostEstimate(flops=10_000_000, bytes_accessed=1_500_000, transcendentals=0),
        name="sum_feat",
    )(parts)


def place_kernel(in_ref, self_ref, neigh_ref, head_self_ref, head_neigh_ref):
    for z in range(8):
        lanes = slice(z * 128, (z + 1) * 128)
        self_ref[:, lanes] = in_ref[2 * z, :48].astype(F32)
        neigh_ref[:, lanes] = in_ref[2 * z + 1, :48].astype(F32)
        head_self_ref[:, lanes] = in_ref[z, 48:].astype(F32)[:153]
        head_neigh_ref[:, lanes] = in_ref[8 + z, 48:].astype(F32)[:153]


def place(parts):
    first = jax.ShapeDtypeStruct((48, 1024), F32)
    head = jax.ShapeDtypeStruct((153, 1024), F32)
    return pl.pallas_call(
        place_kernel,
        out_shape=(first, first, head, head),
        in_specs=vmem(1),
        out_specs=tuple(vmem(4)),
        cost_estimate=pl.CostEstimate(flops=1_000_000, bytes_accessed=2_500_000, transcendentals=0),
        name="place",
    )(parts)


def on_device(
    feature_table,
    node_ids,
    neigh_one,
    count_one,
    neigh_two,
    count_two,
    w_one_self,
    w_one_neigh,
    w_two_self,
    w_two_neigh,
    logit_grad,
):
    column = lax.axis_index("x") * 256
    w_local = jnp.concatenate([w_one_self, w_one_neigh], axis=0)
    w_send = w_local.reshape(96, 4, 256).transpose(1, 0, 2)
    w_send = jnp.broadcast_to(w_send[None], (4, 4, 96, 256)).reshape(16, 96, 256)
    w_x = lax.all_to_all(w_send, FEAT, 0, 0, tiled=True).reshape(1536, 256)
    up_y = lax.all_gather(logit_grad[0], "x", axis=0)
    neigh_y = lax.all_gather(neigh_two[0], "x", axis=0)
    count_y = lax.all_gather(count_two[0], "x", axis=0)

    st = lax.all_to_all(gather(node_ids, neigh_one, count_one, feature_table), FEAT, 0, 0, tiled=True)

    w2s_x = lax.dynamic_slice_in_dim(w_two_self.T, column, 256, 1)
    w2n_x = lax.dynamic_slice_in_dim(w_two_neigh.T, column, 256, 1)
    wt, gh, spread, upt = prepare(w_x, up_y, neigh_y, count_y, w2s_x, w2n_x)
    grads, scores = layers(
        st.reshape(1536, 4 * SUB), wt, gh, spread, count_y, upt, jnp.concatenate([w2s_x, w2n_x], axis=1)
    )
    summed = sum_feat(lax.all_to_all(grads, FEAT, 0, 0, tiled=True))
    scores = lax.all_to_all(scores.reshape(4, TGT, 153), "x", 0, 0, tiled=True)
    logits = jnp.sum(scores, axis=0).astype(BF)[None]

    total = jnp.sum(lax.all_to_all(summed, REP, 0, 0, tiled=True), axis=0)
    head = jnp.broadcast_to(total[48:][None], (16, 16, 128))
    head = lax.all_to_all(head, FEAT, 0, 0, tiled=True)[:, :CLS_ROWS].reshape(160, 128)
    final = jnp.concatenate([total[:48], head], axis=0).astype(BF)
    final = lax.all_gather(final, REP, axis=0)
    grad_self, grad_neigh, head_self, head_neigh = place(final)
    return logits, grad_self, grad_neigh, head_self.T, head_neigh.T


def solution(mesh):
    fine = Mesh(np.asarray(mesh.devices).reshape(4, 4, 8, 2), ("y", "x", "z", "c"))
    return jax.shard_map(
        on_device,
        mesh=fine,
        in_specs=(
            P(FEAT, None),
            P(REP, None),
            P(REP, None, None),
            P(REP, None),
            P(REP, None, FEAT),
            P(REP, FEAT),
            P(FEAT, None),
            P(FEAT, None),
            P(),
            P(),
            P(REP, FEAT, None),
        ),
        out_specs=(P(REP, FEAT, None), P(FEAT, None), P(FEAT, None), P(), P()),
        check_vma=False,
    )
```

```python
import functools

import jax
import jax.numpy as jnp
import numpy as np
from jax import lax
from jax.experimental import pallas as pl
from jax.experimental.pallas import tpu as pltpu
from jax.sharding import Mesh, PartitionSpec as P

BF = jnp.bfloat16
F32 = jnp.float32
GELU_C = 0.7978845608028654
FEAT = ("y", "x")
REP = ("z", "c")
SUB = 128
INP = 512
TGT = 64
CHUNK = 512
LISTS = 160
CLS_ROWS = 10


def mm(first, second):
    return jnp.dot(first, second, preferred_element_type=F32)


def mm_nt(first, second):
    return lax.dot_general(first, second, (((1,), (1,)), ((), ())), preferred_element_type=F32)


def vmem(count):
    return [pl.BlockSpec(memory_space=pltpu.VMEM)] * count


def gather_kernel(ids_ref, neigh_ref, count_ref, table_ref, out_ref, turned, rows):
    cols, papers = table_ref.shape

    def turn(step, carry):
        start = pl.multiple_of(step * CHUNK, CHUNK)
        block = table_ref[:, pl.ds(start, CHUNK)].astype(F32)
        turned[pl.ds(start, CHUNK), :cols] = block.T
        return carry

    lax.fori_loop(0, papers // CHUNK, turn, 0, unroll=2)

    position = lax.broadcasted_iota(jnp.int32, (INP // 2, SUB), 0).astype(F32).astype(BF)
    one = jnp.ones((INP // 2, SUB), BF)
    zero = jnp.zeros((INP // 2, SUB), BF)

    def sub_batch(g, carry):
        base = g * INP
        for j in range(INP):
            rows[pl.ds(j, 1), :] = turned[pl.ds(ids_ref[0, base + j], 1), :]
        nodes = pl.ds(pl.multiple_of(g * SUB, SUB), SUB)
        count = count_ref[:, nodes]
        halves = [zero, zero]
        for k in range(neigh_ref.shape[1]):
            near = jnp.where(k < count, neigh_ref[0, pl.ds(k, 1), nodes], -1)
            for h in range(2):
                here = (near - h * (INP // 2)).astype(F32).astype(BF)
                halves[h] = halves[h] + jnp.where(position == here, one, zero)
        picked = rows[...].T[:cols].astype(BF)
        summed = mm(picked[:, : INP // 2], halves[0]) + mm(picked[:, INP // 2 :], halves[1])
        agg = (summed / count.astype(F32)).astype(BF)
        own = picked[:, :SUB]
        lanes = pl.ds(pl.multiple_of((g % 4) * SUB, SUB), SUB)
        for x in range(4):
            out_ref[(g // 4) * 4 + x, :cols, lanes] = own
            out_ref[(g // 4) * 4 + x, cols:, lanes] = agg
        return carry

    lax.fori_loop(0, 16, sub_batch, 0)


def gather(node_ids, neigh_one, count_one, feature_table):
    cols, papers = feature_table.shape
    return pl.pallas_call(
        gather_kernel,
        out_shape=jax.ShapeDtypeStruct((16, 2 * cols, 4 * SUB), BF),
        in_specs=[pl.BlockSpec(memory_space=pltpu.SMEM)] + vmem(3),
        out_specs=pl.BlockSpec(memory_space=pltpu.VMEM),
        scratch_shapes=[pltpu.VMEM((papers, 128), F32), pltpu.VMEM((INP, 128), F32)],
        compiler_params=pltpu.CompilerParams(vmem_limit_bytes=48 * 2**20),
        cost_estimate=pl.CostEstimate(flops=30_000_000_000, bytes_accessed=5_000_000, transcendentals=0),
        name="gather",
    )(node_ids, neigh_one, count_one, feature_table)


def pack_kernel(w_self_ref, w_neigh_ref, up_ref, neigh_ref, count_ref, out_ref):
    lists = jnp.concatenate([neigh_ref[...], count_ref[...]], axis=0).astype(F32).T.astype(BF)
    for x in range(4):
        lanes = slice(x * 256, (x + 1) * 256)
        for y in range(4):
            out_ref[4 * y + x, :48] = w_self_ref[:, lanes]
            out_ref[4 * y + x, 48:96] = w_neigh_ref[:, lanes]
            out_ref[4 * y + x, 96:, :153] = up_ref[...]
            out_ref[4 * y + x, 96:, LISTS : LISTS + 26] = lists


def pack(w_self, w_neigh, upstream, neigh, count):
    return pl.pallas_call(
        pack_kernel,
        out_shape=jax.ShapeDtypeStruct((16, 96 + TGT, 256), BF),
        in_specs=vmem(5),
        out_specs=vmem(1)[0],
        cost_estimate=pl.CostEstimate(flops=1_000_000, bytes_accessed=1_500_000, transcendentals=0),
        name="pack",
    )(w_self, w_neigh, upstream, neigh, count)


def prepare_kernel(y_ref, in_ref, w2s_ref, w2n_ref, wt_ref, gh_ref, spread_ref, upt_ref, count_ref):
    wt_ref[...] = jnp.concatenate([in_ref[f, :96] for f in range(16)], axis=0).T
    position = lax.broadcasted_iota(jnp.int32, (SUB, TGT), 0).astype(F32)
    for g in range(4):
        upstream = in_ref[4 * y_ref[0] + g, 96:]
        turned = upstream.astype(F32).T
        count = turned[LISTS + 25 : LISTS + 26]
        spread = jnp.zeros((SUB, TGT), F32)
        for k in range(25):
            near = jnp.where(k < count, turned[LISTS + k : LISTS + k + 1], -1.0)
            spread = spread + jnp.where(position == near, 1.0, 0.0)
        spread = spread.astype(BF)
        spread_ref[g] = spread
        own = mm(upstream[:, :153], w2s_ref[...])
        near_grad = mm(upstream[:, :153], w2n_ref[...]).T / count
        high = near_grad.astype(BF)
        low = (near_grad - high.astype(F32)).astype(BF)
        grad = mm_nt(high, spread) + mm_nt(low, spread)
        gh_ref[:, g * SUB : (g + 1) * SUB] = grad + jnp.concatenate([own.T, jnp.zeros(own.T.shape, F32)], axis=1)
        upt_ref[:153, g * TGT : (g + 1) * TGT] = turned[:153].astype(BF)
        count_ref[pl.ds(g, 1), :] = count
    upt_ref[153:] = jnp.zeros((7, 4 * TGT), BF)


def prepare(row, received, w2s_x, w2n_x):
    return pl.pallas_call(
        prepare_kernel,
        out_shape=(
            jax.ShapeDtypeStruct((256, 1536), BF),
            jax.ShapeDtypeStruct((256, 4 * SUB), F32),
            jax.ShapeDtypeStruct((4, SUB, TGT), BF),
            jax.ShapeDtypeStruct((160, 4 * TGT), BF),
            jax.ShapeDtypeStruct((4, TGT), F32),
        ),
        in_specs=[pl.BlockSpec(memory_space=pltpu.SMEM)] + vmem(3),
        out_specs=tuple(vmem(5)),
        cost_estimate=pl.CostEstimate(flops=6_000_000_000, bytes_accessed=2_000_000, transcendentals=0),
        name="prepare",
    )(row, received, w2s_x, w2n_x)


def layers_kernel(x_ref, st_ref, wt_ref, gh_ref, spread_ref, count_ref, upt_ref, w2_ref, grads_ref, *scores_refs):
    pre = mm(wt_ref[...], st_ref[...])
    square = pre * pre
    bend = jnp.tanh(GELU_C * pre * (1.0 + 0.044715 * square))
    half = 0.5 * (1.0 + bend)
    hidden = (pre * half).astype(BF)
    slope = half + 0.5 * pre * (1.0 - bend * bend) * (GELU_C * (1.0 + 3.0 * 0.044715 * square))
    grad_pre = (gh_ref[...] * slope).astype(BF)
    grad = mm_nt(st_ref[...], grad_pre).astype(BF)
    rows = grad.shape[0] // 16
    for f in range(16):
        grads_ref[f, :rows] = grad[f * rows : (f + 1) * rows]
    own, near = [], []
    for g in range(4):
        nodes = hidden[:, g * SUB : (g + 1) * SUB]
        own.append(nodes[:, :TGT])
        near.append((mm(nodes, spread_ref[g]) / count_ref[pl.ds(g, 1), :]).astype(BF))
    both = jnp.concatenate([jnp.concatenate(own, axis=1), jnp.concatenate(near, axis=1)], axis=0)
    scores = mm(w2_ref[...], both).T
    for g in range(4):
        for step, scores_ref in enumerate(scores_refs):

            @pl.when(lax.rem(x_ref[0] + step, 4) == g)
            def _():
                scores_ref[...] = scores[g * TGT : (g + 1) * TGT]

    head = mm_nt(upt_ref[...], both)
    for f in range(16):
        part = head[f * CLS_ROWS : (f + 1) * CLS_ROWS].astype(BF)
        grads_ref[f, 96 : 96 + CLS_ROWS] = part[:, :256]
        grads_ref[f, 112 : 112 + CLS_ROWS] = part[:, 256:]
        grads_ref[f, 96 + CLS_ROWS : 112] = jnp.zeros((16 - CLS_ROWS, 256), BF)
        grads_ref[f, 112 + CLS_ROWS :] = jnp.zeros((16 - CLS_ROWS, 256), BF)


def layers(column, st, wt, gh, spread, count_y, upt, w2_x):
    return pl.pallas_call(
        layers_kernel,
        out_shape=(
            jax.ShapeDtypeStruct((16, 128, 256), BF),
            *[jax.ShapeDtypeStruct((TGT, 153), F32)] * 4,
        ),
        in_specs=[pl.BlockSpec(memory_space=pltpu.SMEM)] + vmem(7),
        out_specs=tuple(vmem(5)),
        cost_estimate=pl.CostEstimate(flops=6_000_000_000, bytes_accessed=4_000_000, transcendentals=200_000),
        name="layers",
    )(column, st, wt, gh, spread, count_y, upt, w2_x)


def sum_feat_kernel(in_ref, out_ref):
    for x in range(4):
        total = sum(in_ref[4 * y + x].astype(F32) for y in range(4))
        for h in range(2):
            half = total[:, h * 128 : (h + 1) * 128]
            z = 2 * x + h
            out_ref[2 * z, :48] = half[:48]
            out_ref[2 * z + 1, :48] = half[48:96]
            out_ref[z, 48:] = half[96:112]
            out_ref[8 + z, 48:] = half[112:]


def sum_feat(parts):
    return pl.pallas_call(
        sum_feat_kernel,
        out_shape=jax.ShapeDtypeStruct((16, 64, 128), F32),
        in_specs=vmem(1),
        out_specs=vmem(1)[0],
        cost_estimate=pl.CostEstimate(flops=10_000_000, bytes_accessed=1_500_000, transcendentals=0),
        name="sum_feat",
    )(parts)


def place_kernel(in_ref, score0, score1, score2, score3, logits_ref, self_ref, neigh_ref, head_self_ref, head_neigh_ref):
    logits_ref[...] = (score0[...] + score1[...] + score2[...] + score3[...]).astype(BF)
    for z in range(8):
        lanes = slice(z * 128, (z + 1) * 128)
        self_ref[:, lanes] = in_ref[2 * z, :48].astype(F32)
        neigh_ref[:, lanes] = in_ref[2 * z + 1, :48].astype(F32)
        head_self_ref[:, lanes] = in_ref[z, 48:].astype(F32)[:153]
        head_neigh_ref[:, lanes] = in_ref[8 + z, 48:].astype(F32)[:153]


def place(parts, scores):
    first = jax.ShapeDtypeStruct((48, 1024), F32)
    head = jax.ShapeDtypeStruct((153, 1024), F32)
    return pl.pallas_call(
        place_kernel,
        out_shape=(jax.ShapeDtypeStruct((TGT, 153), BF), first, first, head, head),
        in_specs=vmem(5),
        out_specs=tuple(vmem(5)),
        cost_estimate=pl.CostEstimate(flops=1_000_000, bytes_accessed=2_500_000, transcendentals=0),
        name="place",
    )(parts, *scores)


def on_device(
    feature_table,
    node_ids,
    neigh_one,
    count_one,
    neigh_two,
    count_two,
    w_one_self,
    w_one_neigh,
    w_two_self,
    w_two_neigh,
    logit_grad,
):
    column = lax.axis_index("x") * 256
    sent = pack(w_one_self, w_one_neigh, logit_grad[0], neigh_two[0], count_two)
    received = lax.all_to_all(sent, FEAT, 0, 0, tiled=True)

    st = lax.all_to_all(gather(node_ids, neigh_one, count_one, feature_table), FEAT, 0, 0, tiled=True)

    w2s_x = lax.dynamic_slice_in_dim(w_two_self.T, column, 256, 1)
    w2n_x = lax.dynamic_slice_in_dim(w_two_neigh.T, column, 256, 1)
    row = lax.axis_index("y").reshape(1)
    wt, gh, spread, upt, count_y = prepare(row, received, w2s_x, w2n_x)
    grads, *scores = layers(
        lax.axis_index("x").reshape(1), st.reshape(1536, 4 * SUB), wt, gh, spread, count_y, upt, jnp.concatenate([w2s_x, w2n_x], axis=1)
    )
    summed = sum_feat(lax.all_to_all(grads, FEAT, 0, 0, tiled=True))
    for step in (1, 2, 3):
        scores[step] = lax.ppermute(scores[step], "x", [(i, (i + step) % 4) for i in range(4)])

    total = jnp.sum(lax.all_to_all(summed, REP, 0, 0, tiled=True), axis=0)
    head = jnp.broadcast_to(total[48:][None], (16, 16, 128))
    head = lax.all_to_all(head, FEAT, 0, 0, tiled=True)[:, :CLS_ROWS].reshape(160, 128)
    final = jnp.concatenate([total[:48], head], axis=0).astype(BF)
    final = lax.all_gather(final, REP, axis=0)
    logits, grad_self, grad_neigh, head_self, head_neigh = place(final, scores)
    return logits[None], grad_self, grad_neigh, head_self.T, head_neigh.T


def solution(mesh):
    fine = Mesh(np.asarray(mesh.devices).reshape(4, 4, 8, 2), ("y", "x", "z", "c"))
    return jax.shard_map(
        on_device,
        mesh=fine,
        in_specs=(
            P(FEAT, None),
            P(REP, None),
            P(REP, None, None),
            P(REP, None),
            P(REP, None, FEAT),
            P(REP, FEAT),
            P(FEAT, None),
            P(FEAT, None),
            P(),
            P(),
            P(REP, FEAT, None),
        ),
        out_specs=(P(REP, FEAT, None), P(FEAT, None), P(FEAT, None), P(), P()),
        check_vma=False,
    )
```

```python
import functools

import jax
import jax.numpy as jnp
import numpy as np
from jax import lax
from jax.experimental import pallas as pl
from jax.experimental.pallas import tpu as pltpu
from jax.sharding import Mesh, PartitionSpec as P

BF = jnp.bfloat16
F32 = jnp.float32
GELU_C = 0.7978845608028654
FEAT = ("y", "x")
REP = ("z", "c")
SUB = 128
INP = 512
TGT = 64
CHUNK = 512
LISTS = 160
CLS_ROWS = 20
CLS_PAD = 24
PIECE = 128


def mm(first, second):
    return jnp.dot(first, second, preferred_element_type=F32)


def mm_nt(first, second):
    return lax.dot_general(first, second, (((1,), (1,)), ((), ())), preferred_element_type=F32)


def vmem(count):
    return [pl.BlockSpec(memory_space=pltpu.VMEM)] * count


def gather_kernel(ids_ref, neigh_ref, count_ref, table_ref, out_ref, turned, rows):
    cols, papers = table_ref.shape

    def turn(step, carry):
        start = pl.multiple_of(step * CHUNK, CHUNK)
        block = table_ref[:, pl.ds(start, CHUNK)].astype(F32)
        turned[pl.ds(start, CHUNK), :cols] = block.T
        return carry

    lax.fori_loop(0, papers // CHUNK, turn, 0, unroll=2)

    position = lax.broadcasted_iota(jnp.int32, (INP // 2, SUB), 0).astype(F32).astype(BF)
    one = jnp.ones((INP // 2, SUB), BF)
    zero = jnp.zeros((INP // 2, SUB), BF)

    def sub_batch(g, carry):
        base = g * INP
        for j in range(INP):
            rows[pl.ds(j, 1), :] = turned[pl.ds(ids_ref[0, base + j], 1), :]
        nodes = pl.ds(pl.multiple_of(g * SUB, SUB), SUB)
        count = count_ref[:, nodes]
        halves = [zero, zero]
        for k in range(neigh_ref.shape[1]):
            near = jnp.where(k < count, neigh_ref[0, pl.ds(k, 1), nodes], -1)
            for h in range(2):
                here = (near - h * (INP // 2)).astype(F32).astype(BF)
                halves[h] = halves[h] + jnp.where(position == here, one, zero)
        picked = rows[...].T[:cols].astype(BF)
        summed = mm(picked[:, : INP // 2], halves[0]) + mm(picked[:, INP // 2 :], halves[1])
        agg = (summed / count.astype(F32)).astype(BF)
        own = picked[:, :SUB]
        lanes = pl.ds(pl.multiple_of((g % 4) * SUB, SUB), SUB)
        for x in range(4):
            out_ref[(g // 4) * 4 + x, :cols, lanes] = own
            out_ref[(g // 4) * 4 + x, cols:, lanes] = agg
        return carry

    lax.fori_loop(0, 16, sub_batch, 0)


def gather(node_ids, neigh_one, count_one, feature_table):
    cols, papers = feature_table.shape
    return pl.pallas_call(
        gather_kernel,
        out_shape=jax.ShapeDtypeStruct((16, 2 * cols, 4 * SUB), BF),
        in_specs=[pl.BlockSpec(memory_space=pltpu.SMEM)] + vmem(3),
        out_specs=pl.BlockSpec(memory_space=pltpu.VMEM),
        scratch_shapes=[pltpu.VMEM((papers, 128), F32), pltpu.VMEM((INP, 128), F32)],
        compiler_params=pltpu.CompilerParams(vmem_limit_bytes=48 * 2**20),
        cost_estimate=pl.CostEstimate(flops=30_000_000_000, bytes_accessed=5_000_000, transcendentals=0),
        name="gather",
    )(node_ids, neigh_one, count_one, feature_table)


def pack_kernel(w_self_ref, w_neigh_ref, up_ref, neigh_ref, count_ref, out_ref):
    lists = jnp.concatenate([neigh_ref[...], count_ref[...]], axis=0).astype(F32).T.astype(BF)
    for x in range(4):
        lanes = slice(x * 256, (x + 1) * 256)
        for y in range(4):
            out_ref[4 * y + x, :48] = w_self_ref[:, lanes]
            out_ref[4 * y + x, 48:96] = w_neigh_ref[:, lanes]
            out_ref[4 * y + x, 96:, :153] = up_ref[...]
            out_ref[4 * y + x, 96:, LISTS : LISTS + 26] = lists


def pack(w_self, w_neigh, upstream, neigh, count):
    return pl.pallas_call(
        pack_kernel,
        out_shape=jax.ShapeDtypeStruct((16, 96 + TGT, 256), BF),
        in_specs=vmem(5),
        out_specs=vmem(1)[0],
        cost_estimate=pl.CostEstimate(flops=1_000_000, bytes_accessed=1_500_000, transcendentals=0),
        name="pack",
    )(w_self, w_neigh, upstream, neigh, count)


def prepare_kernel(y_ref, in_ref, w2s_ref, w2n_ref, wt_ref, gh_ref, spread_ref, upt_ref, count_ref):
    wt_ref[...] = jnp.concatenate([in_ref[f, :96] for f in range(16)], axis=0).T
    position = lax.broadcasted_iota(jnp.int32, (SUB, TGT), 0).astype(F32)
    classes = []
    for g in range(4):
        upstream = in_ref[4 * y_ref[0] + g, 96:]
        turned = upstream.astype(F32).T
        count = turned[LISTS + 25 : LISTS + 26]
        spread = jnp.zeros((SUB, TGT), F32)
        for k in range(25):
            near = jnp.where(k < count, turned[LISTS + k : LISTS + k + 1], -1.0)
            spread = spread + jnp.where(position == near, 1.0, 0.0)
        spread = spread.astype(BF)
        spread_ref[g] = spread
        own = mm(upstream[:, :153], w2s_ref[...])
        near_grad = mm(upstream[:, :153], w2n_ref[...]).T / count
        high = near_grad.astype(BF)
        low = (near_grad - high.astype(F32)).astype(BF)
        grad = mm_nt(high, spread) + mm_nt(low, spread)
        gh_ref[:, g * SUB : (g + 1) * SUB] = grad + jnp.concatenate([own.T, jnp.zeros(own.T.shape, F32)], axis=1)
        classes.append(turned[:153])
        count_ref[pl.ds(g, 1), :] = count
    classes = jnp.concatenate(classes, axis=1)
    blocks = []
    for z in range(8):
        block = classes[z * CLS_ROWS : min((z + 1) * CLS_ROWS, 153)]
        blocks += [block, jnp.zeros((CLS_PAD - block.shape[0], 4 * TGT), F32)]
    upt_ref[...] = jnp.concatenate(blocks, axis=0).astype(BF)


def prepare(row, received, w2s_x, w2n_x):
    return pl.pallas_call(
        prepare_kernel,
        out_shape=(
            jax.ShapeDtypeStruct((256, 1536), BF),
            jax.ShapeDtypeStruct((256, 4 * SUB), F32),
            jax.ShapeDtypeStruct((4, SUB, TGT), BF),
            jax.ShapeDtypeStruct((8 * CLS_PAD, 4 * TGT), BF),
            jax.ShapeDtypeStruct((4, TGT), F32),
        ),
        in_specs=[pl.BlockSpec(memory_space=pltpu.SMEM)] + vmem(3),
        out_specs=tuple(vmem(5)),
        cost_estimate=pl.CostEstimate(flops=6_000_000_000, bytes_accessed=2_000_000, transcendentals=0),
        name="prepare",
    )(row, received, w2s_x, w2n_x)


def layers_kernel(place_ref, st_ref, wt_ref, gh_ref, spread_ref, count_ref, upt_ref, w2_ref, keep_ref, send_ref, *scores_refs):
    pre = mm(wt_ref[...], st_ref[...])
    square = pre * pre
    bend = jnp.tanh(GELU_C * pre * (1.0 + 0.044715 * square))
    half = 0.5 * (1.0 + bend)
    hidden = (pre * half).astype(BF)
    slope = half + 0.5 * pre * (1.0 - bend * bend) * (GELU_C * (1.0 + 3.0 * 0.044715 * square))
    grad_pre = (gh_ref[...] * slope).astype(BF)
    grad = mm_nt(st_ref[...], grad_pre)
    own, near = [], []
    for g in range(4):
        nodes = hidden[:, g * SUB : (g + 1) * SUB]
        own.append(nodes[:, :TGT])
        near.append((mm(nodes, spread_ref[g]) / count_ref[pl.ds(g, 1), :]).astype(BF))
    both = jnp.concatenate([jnp.concatenate(own, axis=1), jnp.concatenate(near, axis=1)], axis=0)
    scores = mm(w2_ref[...], both).T
    for g in range(4):
        for step, scores_ref in enumerate(scores_refs):

            @pl.when(lax.rem(place_ref[0] + step, 4) == g)
            def _():
                scores_ref[...] = scores[g * TGT : (g + 1) * TGT]

    head = mm_nt(upt_ref[...], both)

    def pieces(side):
        for z in range(8):
            rows = []
            for f in range(16):
                tile = (z - 6 * f) % 8
                if tile < 6:
                    start = f * 96 + side * 48 + tile * 8
                    rows.append(grad[start : start + 8])
            rows.append(head[z * CLS_PAD : (z + 1) * CLS_PAD, side * 256 : (side + 1) * 256])
            rows.append(jnp.zeros((PIECE - 96 - CLS_PAD, 256), F32))
            yield z, jnp.concatenate(rows, axis=0)

    for side in range(2):

        @pl.when(place_ref[1] == side)
        def _():
            for z, piece in pieces(side):
                keep_ref[z] = piece
            for z, piece in pieces(1 - side):
                send_ref[z] = piece.astype(BF)


def layers(position, st, wt, gh, spread, count_y, upt, w2_x):
    return pl.pallas_call(
        layers_kernel,
        out_shape=(
            jax.ShapeDtypeStruct((8, PIECE, 256), F32),
            jax.ShapeDtypeStruct((8, PIECE, 256), BF),
            *[jax.ShapeDtypeStruct((TGT, 153), F32)] * 4,
        ),
        in_specs=[pl.BlockSpec(memory_space=pltpu.SMEM)] + vmem(7),
        out_specs=tuple(vmem(6)),
        cost_estimate=pl.CostEstimate(flops=6_000_000_000, bytes_accessed=4_000_000, transcendentals=200_000),
        name="layers",
    )(position, st, wt, gh, spread, count_y, upt, w2_x)


def sum_z_kernel(z_ref, in_ref, out_ref, total):
    total[...] = sum(in_ref[z].astype(F32) for z in range(8))
    absent = 3 - lax.div(z_ref[0], 2)
    for f in range(16):
        slot = (f // 4) * 3 + f % 4 - (f % 4 > absent).astype(jnp.int32)
        own = total[pl.ds(pl.multiple_of(slot * 8, 8), 8), :]
        out_ref[f] = jnp.concatenate([own, total[96 : 96 + CLS_PAD]], axis=0).astype(BF)


def sum_z(z, parts):
    return pl.pallas_call(
        sum_z_kernel,
        out_shape=jax.ShapeDtypeStruct((16, 8 + CLS_PAD, 256), BF),
        in_specs=[pl.BlockSpec(memory_space=pltpu.SMEM)] + vmem(1),
        out_specs=vmem(1)[0],
        scratch_shapes=[pltpu.VMEM((PIECE, 256), F32)],
        cost_estimate=pl.CostEstimate(flops=10_000_000, bytes_accessed=1_500_000, transcendentals=0),
        name="sum_z",
    )(z, parts)


def sum_y_kernel(in_ref, out_ref):
    for x in range(4):
        total = sum(in_ref[4 * y + x].astype(F32) for y in range(4))
        out_ref[:, x * 256 : (x + 1) * 256] = total[: 8 + CLS_ROWS].astype(BF)


def sum_y(parts):
    return pl.pallas_call(
        sum_y_kernel,
        out_shape=jax.ShapeDtypeStruct((8 + CLS_ROWS, 1024), BF),
        in_specs=vmem(1),
        out_specs=vmem(1)[0],
        cost_estimate=pl.CostEstimate(flops=1_000_000, bytes_accessed=600_000, transcendentals=0),
        name="sum_y",
    )(parts)


def place_kernel(x_ref, in_ref, score0, score1, score2, score3, logits_ref, self_ref, neigh_ref, head_self_ref, head_neigh_ref):
    logits_ref[...] = (score0[...] + score1[...] + score2[...] + score3[...]).astype(BF)
    for side, (first_ref, head_ref) in enumerate(((self_ref, head_self_ref), (neigh_ref, head_neigh_ref))):
        for tile in range(6):
            owner = lax.rem(tile + 6 * x_ref[0], 8)
            first_ref[tile * 8 : (tile + 1) * 8] = in_ref[2 * owner + side].astype(F32)[:8]
        for z in range(8):
            end = min((z + 1) * CLS_ROWS, 153)
            head_ref[z * CLS_ROWS : end] = in_ref[2 * z + side].astype(F32)[8 : 8 + end - z * CLS_ROWS]


def place(x, parts, scores):
    first = jax.ShapeDtypeStruct((48, 1024), F32)
    head = jax.ShapeDtypeStruct((153, 1024), F32)
    return pl.pallas_call(
        place_kernel,
        out_shape=(jax.ShapeDtypeStruct((TGT, 153), BF), first, first, head, head),
        in_specs=[pl.BlockSpec(memory_space=pltpu.SMEM)] + vmem(5),
        out_specs=tuple(vmem(5)),
        cost_estimate=pl.CostEstimate(flops=1_000_000, bytes_accessed=2_500_000, transcendentals=0),
        name="place",
    )(x, parts, *scores)


def on_device(
    feature_table,
    node_ids,
    neigh_one,
    count_one,
    neigh_two,
    count_two,
    w_one_self,
    w_one_neigh,
    w_two_self,
    w_two_neigh,
    logit_grad,
):
    column = lax.axis_index("x") * 256
    sent = pack(w_one_self, w_one_neigh, logit_grad[0], neigh_two[0], count_two)
    received = lax.all_to_all(sent, FEAT, 0, 0, tiled=True)

    st = lax.all_to_all(gather(node_ids, neigh_one, count_one, feature_table), FEAT, 0, 0, tiled=True)

    w2s_x = lax.dynamic_slice_in_dim(w_two_self.T, column, 256, 1)
    w2n_x = lax.dynamic_slice_in_dim(w_two_neigh.T, column, 256, 1)
    row = lax.axis_index("y").reshape(1)
    wt, gh, spread, upt, count_y = prepare(row, received, w2s_x, w2n_x)
    position = jnp.stack([lax.axis_index("x"), lax.axis_index("c")])
    keep, send, *scores = layers(
        position, st.reshape(1536, 4 * SUB), wt, gh, spread, count_y, upt, jnp.concatenate([w2s_x, w2n_x], axis=1)
    )
    for step in (1, 2, 3):
        scores[step] = lax.ppermute(scores[step], "x", [(i, (i + step) % 4) for i in range(4)])

    pair = (keep + lax.ppermute(send, "c", [(0, 1), (1, 0)]).astype(F32)).astype(BF)
    pair, scores = lax.optimization_barrier((lax.all_to_all(pair, "z", 0, 0, tiled=True), scores))
    over_z = sum_z(lax.axis_index("z").reshape(1), pair)
    final = sum_y(lax.all_to_all(over_z, FEAT, 0, 0, tiled=True))
    final = lax.all_gather(final, REP, axis=0)
    logits, grad_self, grad_neigh, head_self, head_neigh = place(position[:1], final, scores)
    return logits[None], grad_self, grad_neigh, head_self.T, head_neigh.T


def solution(mesh):
    fine = Mesh(np.asarray(mesh.devices).reshape(4, 4, 8, 2), ("y", "x", "z", "c"))
    return jax.shard_map(
        on_device,
        mesh=fine,
        in_specs=(
            P(FEAT, None),
            P(REP, None),
            P(REP, None, None),
            P(REP, None),
            P(REP, None, FEAT),
            P(REP, FEAT),
            P(FEAT, None),
            P(FEAT, None),
            P(),
            P(),
            P(REP, FEAT, None),
        ),
        out_specs=(P(REP, FEAT, None), P(FEAT, None), P(FEAT, None), P(), P()),
        check_vma=False,
    )
```

```python
import functools

import jax
import jax.numpy as jnp
import numpy as np
from jax import lax
from jax.experimental import pallas as pl
from jax.experimental.pallas import tpu as pltpu
from jax.sharding import Mesh, PartitionSpec as P

BF = jnp.bfloat16
F32 = jnp.float32
GELU_C = 0.7978845608028654
SMALL = pltpu.CompilerParams(vmem_limit_bytes=8 * 2**20)
FEAT = ("y", "x")
REP = ("z", "c")
SUB = 128
INP = 512
TGT = 64
CHUNK = 4096
LISTS = 160
CLS_ROWS = 20
CLS_PAD = 24
PIECE = 128


def mm(first, second):
    return jnp.dot(first, second, preferred_element_type=F32)


def mm_nt(first, second):
    return lax.dot_general(first, second, (((1,), (1,)), ((), ())), preferred_element_type=F32)


def vmem(count):
    return [pl.BlockSpec(memory_space=pltpu.VMEM)] * count


def gather_kernel(ids_ref, neigh_ref, count_ref, table_ref, out_ref, turned, even, odd):
    cols, papers = table_ref.shape
    fan = neigh_ref.shape[0]
    share = -(-INP // (fan + 1))

    def turn(step, carry):
        start = pl.multiple_of(step * CHUNK, CHUNK)
        turned[pl.ds(start, CHUNK), :cols] = table_ref[:, pl.ds(start, CHUNK)].T.astype(F32)
        return carry

    lax.fori_loop(0, papers // CHUNK, turn, 0)

    position = lax.broadcasted_iota(jnp.int32, (INP // 2, SUB), 0).astype(F32).astype(BF)
    one = jnp.ones((INP // 2, SUB), BF)
    zero = jnp.zeros((INP // 2, SUB), BF)

    def fetch(g, rows, first, last):
        for j in range(first, last):
            rows[pl.ds(j, 1), :] = turned[pl.ds(ids_ref[0, g * INP + j], 1), :]

    def sub_batch(g, rows, later, later_rows):
        nodes = pl.ds(pl.multiple_of(g * SUB, SUB), SUB)
        count = count_ref[:, nodes]
        halves = [zero, zero]
        for k in range(fan):
            fetch(later, later_rows, k * share, (k + 1) * share)
            near = jnp.where(k < count, neigh_ref[k, :, nodes], -1)
            for h in range(2):
                here = (near - h * (INP // 2)).astype(F32).astype(BF)
                halves[h] = halves[h] + jnp.where(position == here, one, zero)
        fetch(later, later_rows, fan * share, INP)
        picked = rows[...].astype(BF).T[:cols]
        summed = mm(picked[:, : INP // 2], halves[0]) + mm(picked[:, INP // 2 :], halves[1])
        agg = (summed / count.astype(F32)).astype(BF)
        own = picked[:, :SUB]
        lanes = pl.ds(pl.multiple_of((g % 4) * SUB, SUB), SUB)
        for x in range(4):
            out_ref[(g // 4) * 4 + x, :cols, lanes] = own
            out_ref[(g // 4) * 4 + x, cols:, lanes] = agg

    fetch(0, even, 0, INP)

    def pair(step, carry):
        sub_batch(2 * step, even, 2 * step + 1, odd)
        sub_batch(2 * step + 1, odd, jnp.minimum(2 * step + 2, 15), even)
        return carry

    lax.fori_loop(0, 8, pair, 0)


def gather(node_ids, neigh_one, count_one, feature_table):
    cols, papers = feature_table.shape
    return pl.pallas_call(
        gather_kernel,
        out_shape=jax.ShapeDtypeStruct((16, 2 * cols, 4 * SUB), BF),
        in_specs=[pl.BlockSpec(memory_space=pltpu.SMEM)] + vmem(3),
        out_specs=pl.BlockSpec(memory_space=pltpu.VMEM),
        scratch_shapes=[pltpu.VMEM((papers, 128), F32), pltpu.VMEM((INP, 128), F32), pltpu.VMEM((INP, 128), F32)],
        compiler_params=pltpu.CompilerParams(vmem_limit_bytes=40 * 2**20),
        cost_estimate=pl.CostEstimate(flops=30_000_000_000, bytes_accessed=5_000_000, transcendentals=0),
        name="gather",
    )(node_ids, neigh_one, count_one, feature_table)


def pack_kernel(w_self_ref, w_neigh_ref, up_ref, neigh_ref, count_ref, out_ref):
    lists = jnp.concatenate([neigh_ref[...], count_ref[...], jnp.zeros((6, TGT), jnp.int32)], axis=0).astype(F32)
    turned = jnp.concatenate([up_ref[...].astype(F32).T, jnp.zeros((7, TGT), F32), lists], axis=0)
    target = jnp.concatenate([turned[k * 48 : (k + 1) * 48] for k in range(4)], axis=1).astype(BF)
    for x in range(4):
        lanes = slice(x * 256, (x + 1) * 256)
        for y in range(4):
            out_ref[4 * y + x, :48] = w_self_ref[:, lanes]
            out_ref[4 * y + x, 48:96] = w_neigh_ref[:, lanes]
            out_ref[4 * y + x, 96:] = target


def pack(w_self, w_neigh, upstream, neigh, count):
    return pl.pallas_call(
        pack_kernel,
        out_shape=jax.ShapeDtypeStruct((16, 144, 256), BF),
        in_specs=vmem(5),
        out_specs=vmem(1)[0],
        cost_estimate=pl.CostEstimate(flops=1_000_000, bytes_accessed=1_500_000, transcendentals=0),
        name="pack",
    )(w_self, w_neigh, upstream, neigh, count)


def prepare_kernel(y_ref, in_ref, w2s_ref, w2n_ref, wt_ref, gh_ref, spread_ref, upt_ref, count_ref):
    wt_ref[...] = jnp.concatenate([in_ref[f, :96] for f in range(16)], axis=0).T
    position = lax.broadcasted_iota(jnp.int32, (SUB, TGT), 0).astype(F32)
    classes = []
    for g in range(4):
        target = in_ref[4 * y_ref[0] + g, 96:].astype(F32)
        turned = jnp.concatenate([target[:, k * TGT : (k + 1) * TGT] for k in range(4)], axis=0)
        upstream = turned[:153].T.astype(BF)
        count = turned[LISTS + 25 : LISTS + 26]
        spread = jnp.zeros((SUB, TGT), F32)
        for k in range(25):
            near = jnp.where(k < count, turned[LISTS + k : LISTS + k + 1], -1.0)
            spread = spread + jnp.where(position == near, 1.0, 0.0)
        spread = spread.astype(BF)
        spread_ref[g] = spread
        own = mm(upstream, w2s_ref[...])
        near_grad = mm(upstream, w2n_ref[...]).T / count
        high = near_grad.astype(BF)
        low = (near_grad - high.astype(F32)).astype(BF)
        grad = mm_nt(high, spread) + mm_nt(low, spread)
        gh_ref[:, g * SUB : (g + 1) * SUB] = grad + jnp.concatenate([own.T, jnp.zeros(own.T.shape, F32)], axis=1)
        classes.append(turned[:153])
        count_ref[pl.ds(g, 1), :] = count
    classes = jnp.concatenate(classes, axis=1)
    blocks = []
    for z in range(8):
        block = classes[z * CLS_ROWS : min((z + 1) * CLS_ROWS, 153)]
        blocks += [block, jnp.zeros((CLS_PAD - block.shape[0], 4 * TGT), F32)]
    upt_ref[...] = jnp.concatenate(blocks, axis=0).astype(BF)


def prepare(y, received, w2s_x, w2n_x):
    return pl.pallas_call(
        prepare_kernel,
        out_shape=(
            jax.ShapeDtypeStruct((256, 1536), BF),
            jax.ShapeDtypeStruct((256, 4 * SUB), F32),
            jax.ShapeDtypeStruct((4, SUB, TGT), BF),
            jax.ShapeDtypeStruct((8 * CLS_PAD, 4 * TGT), BF),
            jax.ShapeDtypeStruct((4, TGT), F32),
        ),
        in_specs=[pl.BlockSpec(memory_space=pltpu.SMEM)] + vmem(3),
        out_specs=tuple(vmem(5)),
        cost_estimate=pl.CostEstimate(flops=6_000_000_000, bytes_accessed=2_000_000, transcendentals=0),
        compiler_params=SMALL,
        name="prepare",
    )(y, received, w2s_x, w2n_x)


def layers_kernel(place_ref, st_ref, wt_ref, gh_ref, spread_ref, count_ref, upt_ref, w2_ref, keep_ref, send_ref, *scores_refs):
    pre = mm(wt_ref[...], st_ref[...])
    square = pre * pre
    bend = jnp.tanh(GELU_C * pre * (1.0 + 0.044715 * square))
    half = 0.5 * (1.0 + bend)
    hidden = (pre * half).astype(BF)
    slope = half + 0.5 * pre * (1.0 - bend * bend) * (GELU_C * (1.0 + 3.0 * 0.044715 * square))
    grad_pre = (gh_ref[...] * slope).astype(BF)
    grad = mm_nt(st_ref[...], grad_pre)
    own, near = [], []
    for g in range(4):
        nodes = hidden[:, g * SUB : (g + 1) * SUB]
        own.append(nodes[:, :TGT])
        near.append((mm(nodes, spread_ref[g]) / count_ref[pl.ds(g, 1), :]).astype(BF))
    both = jnp.concatenate([jnp.concatenate(own, axis=1), jnp.concatenate(near, axis=1)], axis=0)
    scores = mm(w2_ref[...], both).T
    for g in range(4):
        for step, scores_ref in enumerate(scores_refs):

            @pl.when(lax.rem(place_ref[0] + step, 4) == g)
            def _():
                scores_ref[...] = scores[g * TGT : (g + 1) * TGT]

    head = mm_nt(upt_ref[...], both)

    def pieces(side):
        for z in range(8):
            rows = []
            for f in range(16):
                tile = (z - 6 * f) % 8
                if tile < 6:
                    start = f * 96 + side * 48 + tile * 8
                    rows.append(grad[start : start + 8])
            rows.append(head[z * CLS_PAD : (z + 1) * CLS_PAD, side * 256 : (side + 1) * 256])
            rows.append(jnp.zeros((PIECE - 96 - CLS_PAD, 256), F32))
            yield z, jnp.concatenate(rows, axis=0)

    for side in range(2):

        @pl.when(place_ref[1] == side)
        def _():
            for z, piece in pieces(side):
                keep_ref[z] = piece
            for z, piece in pieces(1 - side):
                send_ref[z] = piece.astype(BF)


def layers(position, st, wt, gh, spread, count_y, upt, w2_x):
    return pl.pallas_call(
        layers_kernel,
        out_shape=(
            jax.ShapeDtypeStruct((8, PIECE, 256), F32),
            jax.ShapeDtypeStruct((8, PIECE, 256), BF),
            *[jax.ShapeDtypeStruct((TGT, 153), F32)] * 4,
        ),
        in_specs=[pl.BlockSpec(memory_space=pltpu.SMEM)] + vmem(7),
        out_specs=tuple(vmem(6)),
        cost_estimate=pl.CostEstimate(flops=6_000_000_000, bytes_accessed=4_000_000, transcendentals=200_000),
        compiler_params=SMALL,
        name="layers",
    )(position, st, wt, gh, spread, count_y, upt, w2_x)


def add_pair_kernel(keep_ref, came_ref, out_ref):
    for z in range(8):
        out_ref[z] = (keep_ref[z] + came_ref[z].astype(F32)).astype(BF)


def add_pair(keep, came):
    return pl.pallas_call(
        add_pair_kernel,
        out_shape=jax.ShapeDtypeStruct(came.shape, BF),
        in_specs=vmem(2),
        out_specs=vmem(1)[0],
        cost_estimate=pl.CostEstimate(flops=1_000_000, bytes_accessed=2_000_000, transcendentals=0),
        compiler_params=SMALL,
        name="add_pair",
    )(keep, came)


def sum_z_kernel(z_ref, in_ref, out_ref, total):
    total[...] = sum(in_ref[z].astype(F32) for z in range(8))
    absent = 3 - lax.div(z_ref[0], 2)
    for f in range(16):
        slot = (f // 4) * 3 + f % 4 - (f % 4 > absent).astype(jnp.int32)
        own = total[pl.ds(pl.multiple_of(slot * 8, 8), 8), :]
        out_ref[f] = jnp.concatenate([own, total[96 : 96 + CLS_PAD]], axis=0).astype(BF)


def sum_z(z, parts):
    return pl.pallas_call(
        sum_z_kernel,
        out_shape=jax.ShapeDtypeStruct((16, 8 + CLS_PAD, 256), BF),
        in_specs=[pl.BlockSpec(memory_space=pltpu.SMEM)] + vmem(1),
        out_specs=vmem(1)[0],
        scratch_shapes=[pltpu.VMEM((PIECE, 256), F32)],
        cost_estimate=pl.CostEstimate(flops=10_000_000, bytes_accessed=1_500_000, transcendentals=0),
        compiler_params=SMALL,
        name="sum_z",
    )(z, parts)


def sum_y_kernel(in_ref, out_ref):
    for x in range(4):
        total = sum(in_ref[4 * y + x].astype(F32) for y in range(4))
        out_ref[:, x * 256 : (x + 1) * 256] = total[: 8 + CLS_ROWS].astype(BF)


def sum_y(parts):
    return pl.pallas_call(
        sum_y_kernel,
        out_shape=jax.ShapeDtypeStruct((8 + CLS_ROWS, 1024), BF),
        in_specs=vmem(1),
        out_specs=vmem(1)[0],
        cost_estimate=pl.CostEstimate(flops=1_000_000, bytes_accessed=600_000, transcendentals=0),
        compiler_params=SMALL,
        name="sum_y",
    )(parts)


def place_kernel(x_ref, in_ref, score0, score1, score2, score3, logits_ref, self_ref, neigh_ref, head_self_ref, head_neigh_ref):
    logits_ref[...] = (score0[...] + score1[...] + score2[...] + score3[...]).astype(BF)
    for side, (first_ref, head_ref) in enumerate(((self_ref, head_self_ref), (neigh_ref, head_neigh_ref))):
        for tile in range(6):
            owner = lax.rem(tile + 6 * x_ref[0], 8)
            first_ref[tile * 8 : (tile + 1) * 8] = in_ref[2 * owner + side].astype(F32)[:8]
        for z in range(8):
            end = min((z + 1) * CLS_ROWS, 153)
            head_ref[z * CLS_ROWS : end] = in_ref[2 * z + side].astype(F32)[8 : 8 + end - z * CLS_ROWS]


def place(x, parts, scores):
    first = jax.ShapeDtypeStruct((48, 1024), F32)
    head = jax.ShapeDtypeStruct((153, 1024), F32)
    return pl.pallas_call(
        place_kernel,
        out_shape=(jax.ShapeDtypeStruct((TGT, 153), BF), first, first, head, head),
        in_specs=[pl.BlockSpec(memory_space=pltpu.SMEM)] + vmem(5),
        out_specs=tuple(vmem(5)),
        cost_estimate=pl.CostEstimate(flops=1_000_000, bytes_accessed=2_500_000, transcendentals=0),
        compiler_params=SMALL,
        name="place",
    )(x, parts, *scores)


def shifted(parts, axis):
    moves = [[(source, (source + step) % 4) for source in range(4)] for step in range(4)]
    return [parts[0]] + [lax.ppermute(parts[step], axis, moves[step]) for step in (1, 2, 3)]


def on_device(
    feature_table,
    node_ids,
    neigh_one,
    count_one,
    neigh_two,
    count_two,
    w_one_self,
    w_one_neigh,
    w_two_self,
    w_two_neigh,
    logit_grad,
):
    x, y, z, c = [lax.axis_index(axis).reshape(1) for axis in ("x", "y", "z", "c")]
    sent = pack(w_one_self, w_one_neigh, logit_grad[0], neigh_two[0], count_two)
    received = lax.all_to_all(sent, FEAT, 0, 0, tiled=True)
    gathered = gather(node_ids, neigh_one.transpose(1, 0, 2), count_one, feature_table)
    st = lax.all_to_all(gathered, FEAT, 0, 0, tiled=True)

    w2s_x = lax.dynamic_slice_in_dim(w_two_self.T, x[0] * 256, 256, 1)
    w2n_x = lax.dynamic_slice_in_dim(w_two_neigh.T, x[0] * 256, 256, 1)
    wt, gh, spread, upt, count_y = prepare(y, received, w2s_x, w2n_x)
    position = jnp.concatenate([x, c])
    keep, send, *scores = layers(
        position, st.reshape(1536, 4 * SUB), wt, gh, spread, count_y, upt, jnp.concatenate([w2s_x, w2n_x], axis=1)
    )
    scores = shifted(scores, "x")

    pair = add_pair(keep, lax.ppermute(send, "c", [(0, 1), (1, 0)]))
    pair, scores = lax.optimization_barrier((lax.all_to_all(pair, "z", 0, 0, tiled=True), scores))
    over_z = sum_z(z, pair)
    final = sum_y(lax.all_to_all(over_z, FEAT, 0, 0, tiled=True))
    final = lax.all_gather(final, REP, axis=0)
    logits, grad_self, grad_neigh, head_self, head_neigh = place(x, final, scores)
    return logits[None], grad_self, grad_neigh, head_self.T, head_neigh.T


def solution(mesh):
    fine = Mesh(np.asarray(mesh.devices).reshape(4, 4, 8, 2), ("y", "x", "z", "c"))
    return jax.shard_map(
        on_device,
        mesh=fine,
        in_specs=(
            P(FEAT, None),
            P(REP, None),
            P(REP, None, None),
            P(REP, None),
            P(REP, None, FEAT),
            P(REP, FEAT),
            P(FEAT, None),
            P(FEAT, None),
            P(),
            P(),
            P(REP, FEAT, None),
        ),
        out_specs=(P(REP, FEAT, None), P(FEAT, None), P(FEAT, None), P(), P()),
        check_vma=False,
    )
```

```python
import functools

import jax
import jax.numpy as jnp
import numpy as np
from jax import lax
from jax.experimental import pallas as pl
from jax.experimental.pallas import tpu as pltpu
from jax.sharding import Mesh, PartitionSpec as P

BF = jnp.bfloat16
F32 = jnp.float32
GELU_C = 0.7978845608028654
SMALL = pltpu.CompilerParams(vmem_limit_bytes=8 * 2**20)
FEAT = ("y", "x")
REP = ("z", "c")
SUB = 128
INP = 512
TGT = 64
CHUNK = 4096
LISTS = 160
CLS_ROWS = 20
CLS_PAD = 24
PIECE = 120


def mm(first, second):
    return jnp.dot(first, second, preferred_element_type=F32)


def mm_nt(first, second):
    return lax.dot_general(first, second, (((1,), (1,)), ((), ())), preferred_element_type=F32)


def vmem(count):
    return [pl.BlockSpec(memory_space=pltpu.VMEM)] * count


def gather_kernel(ids_ref, neigh_ref, count_ref, table_ref, out_ref, table, turned, even, odd, arrived):
    cols, papers = table_ref.shape
    fan = neigh_ref.shape[0]
    share = -(-INP // (fan + 1))

    blocks = [pl.ds(start, CHUNK) for start in range(0, papers, CHUNK)]
    copies = [
        pltpu.make_async_copy(table_ref.at[:, block], table.at[:, block], arrived.at[at])
        for at, block in enumerate(blocks)
    ]
    for copy in copies:
        copy.start()
    for block, copy in zip(blocks, copies):
        copy.wait()
        turned[block, :cols] = table[:, block].T.astype(F32)

    position = lax.broadcasted_iota(jnp.int32, (INP // 2, SUB), 0).astype(F32).astype(BF)
    one = jnp.ones((INP // 2, SUB), BF)
    zero = jnp.zeros((INP // 2, SUB), BF)

    def fetch(g, rows, first, last):
        for j in range(first, last):
            rows[pl.ds(j, 1), :] = turned[pl.ds(ids_ref[0, g * INP + j], 1), :]

    def sub_batch(g, rows, later, later_rows):
        nodes = pl.ds(pl.multiple_of(g * SUB, SUB), SUB)
        count = count_ref[:, nodes]
        halves = [zero, zero]
        for k in range(fan):
            fetch(later, later_rows, k * share, (k + 1) * share)
            near = jnp.where(k < count, neigh_ref[k, :, nodes], -1)
            for h in range(2):
                here = (near - h * (INP // 2)).astype(F32).astype(BF)
                halves[h] = halves[h] + jnp.where(position == here, one, zero)
        fetch(later, later_rows, fan * share, INP)
        picked = rows[...].astype(BF).T[:cols]
        summed = mm(picked[:, : INP // 2], halves[0]) + mm(picked[:, INP // 2 :], halves[1])
        agg = (summed / count.astype(F32)).astype(BF)
        own = picked[:, :SUB]
        lanes = pl.ds(pl.multiple_of((g % 4) * SUB, SUB), SUB)
        for x in range(4):
            out_ref[(g // 4) * 4 + x, :cols, lanes] = own
            out_ref[(g // 4) * 4 + x, cols:, lanes] = agg

    fetch(0, even, 0, INP)

    def pair(step, carry):
        sub_batch(2 * step, even, 2 * step + 1, odd)
        sub_batch(2 * step + 1, odd, jnp.minimum(2 * step + 2, 15), even)
        return carry

    lax.fori_loop(0, 8, pair, 0)


def gather(node_ids, neigh_one, count_one, feature_table):
    cols, papers = feature_table.shape
    return pl.pallas_call(
        gather_kernel,
        out_shape=jax.ShapeDtypeStruct((16, 2 * cols, 4 * SUB), BF),
        in_specs=[pl.BlockSpec(memory_space=pltpu.SMEM)] + vmem(2) + [pl.BlockSpec(memory_space=pl.ANY)],
        out_specs=pl.BlockSpec(memory_space=pltpu.VMEM),
        scratch_shapes=[
            pltpu.VMEM((cols, papers), BF),
            pltpu.VMEM((papers, 128), F32),
            pltpu.VMEM((INP, 128), F32),
            pltpu.VMEM((INP, 128), F32),
            pltpu.SemaphoreType.DMA((papers // CHUNK,)),
        ],
        compiler_params=pltpu.CompilerParams(vmem_limit_bytes=56 * 2**20),
        cost_estimate=pl.CostEstimate(flops=30_000_000_000, bytes_accessed=5_000_000, transcendentals=0),
        name="gather",
    )(node_ids, neigh_one, count_one, feature_table)


def pack_kernel(c_ref, w_self_ref, w_neigh_ref, up_ref, neigh_ref, count_ref, out_ref):
    near = [neigh_ref[k] for k in range(neigh_ref.shape[0])]
    lists = jnp.concatenate(near + [count_ref[...], jnp.zeros((6, TGT), jnp.int32)], axis=0).astype(F32)
    turned = jnp.concatenate([up_ref[...].astype(F32).T, jnp.zeros((7, TGT), F32), lists], axis=0)
    target = jnp.concatenate([turned[k * 48 : (k + 1) * 48] for k in range(4)], axis=1).astype(BF)
    for x in range(4):
        lanes = slice(x * 256, (x + 1) * 256)
        for y in range(4):
            out_ref[4 * y + x, 48:] = target
            for side, w_ref in enumerate((w_self_ref, w_neigh_ref)):

                @pl.when(c_ref[0] == side)
                def _():
                    out_ref[4 * y + x, :48] = w_ref[:, lanes]


def pack(c, w_self, w_neigh, upstream, neigh, count):
    return pl.pallas_call(
        pack_kernel,
        out_shape=jax.ShapeDtypeStruct((16, 96, 256), BF),
        in_specs=[pl.BlockSpec(memory_space=pltpu.SMEM)] + vmem(5),
        out_specs=vmem(1)[0],
        cost_estimate=pl.CostEstimate(flops=1_000_000, bytes_accessed=1_500_000, transcendentals=0),
        name="pack",
    )(c, w_self, w_neigh, upstream, neigh, count)


def turn_weights_kernel(place_ref, in_ref, came_ref, wt_ref, targets_ref):
    for side in range(2):

        @pl.when(place_ref[1] == side)
        def _():
            sides = (in_ref, came_ref) if side == 0 else (came_ref, in_ref)
            wt_ref[...] = jnp.concatenate([ref[f, :48] for f in range(16) for ref in sides], axis=0).T

    for g in range(4):
        targets_ref[g] = in_ref[4 * place_ref[0] + g, 48:]


def turn_weights(position, received, came):
    return pl.pallas_call(
        turn_weights_kernel,
        out_shape=(jax.ShapeDtypeStruct((256, 1536), BF), jax.ShapeDtypeStruct((4, 48, 256), BF)),
        in_specs=[pl.BlockSpec(memory_space=pltpu.SMEM)] + vmem(2),
        out_specs=tuple(vmem(2)),
        cost_estimate=pl.CostEstimate(flops=1_000_000, bytes_accessed=2_000_000, transcendentals=0),
        compiler_params=SMALL,
        name="turn_weights",
    )(position, received, came)


def layers_kernel(place_ref, st_ref, wt_ref, targets_ref, w2s_ref, w2n_ref, keep_ref, send_ref, *scores_refs):
    position = lax.broadcasted_iota(jnp.int32, (SUB, TGT), 0).astype(F32)
    classes, spreads, hidden_grads, counts = [], [], [], []
    for g in range(4):
        target = targets_ref[g].astype(F32)
        turned = jnp.concatenate([target[:, k * TGT : (k + 1) * TGT] for k in range(4)], axis=0)
        upstream = turned[:153].T.astype(BF)
        count = turned[LISTS + 25 : LISTS + 26]
        spread = jnp.zeros((SUB, TGT), F32)
        for k in range(25):
            near = jnp.where(k < count, turned[LISTS + k : LISTS + k + 1], -1.0)
            spread = spread + jnp.where(position == near, 1.0, 0.0)
        spread = spread.astype(BF)
        spreads.append(spread)
        own = mm(upstream, w2s_ref[...])
        near_grad = mm(upstream, w2n_ref[...]).T / count
        high = near_grad.astype(BF)
        low = (near_grad - high.astype(F32)).astype(BF)
        grad = mm_nt(high, spread) + mm_nt(low, spread)
        hidden_grads.append(grad + jnp.concatenate([own.T, jnp.zeros(own.T.shape, F32)], axis=1))
        classes.append(turned[:153])
        counts.append(count)
    classes = jnp.concatenate(classes, axis=1)
    blocks = []
    for z in range(8):
        block = classes[z * CLS_ROWS : min((z + 1) * CLS_ROWS, 153)]
        blocks += [block, jnp.zeros((CLS_PAD - block.shape[0], 4 * TGT), F32)]
    classes = jnp.concatenate(blocks, axis=0).astype(BF)

    pre = mm(wt_ref[...], st_ref[...])
    square = pre * pre
    bend = jnp.tanh(GELU_C * pre * (1.0 + 0.044715 * square))
    half = 0.5 * (1.0 + bend)
    hidden = (pre * half).astype(BF)
    slope = half + 0.5 * pre * (1.0 - bend * bend) * (GELU_C * (1.0 + 3.0 * 0.044715 * square))
    grad_pre = (jnp.concatenate(hidden_grads, axis=1) * slope).astype(BF)
    grad = mm_nt(st_ref[...], grad_pre)
    own, near = [], []
    for g in range(4):
        nodes = hidden[:, g * SUB : (g + 1) * SUB]
        own.append(nodes[:, :TGT])
        near.append((mm(nodes, spreads[g]) / counts[g]).astype(BF))
    both = jnp.concatenate([jnp.concatenate(own, axis=1), jnp.concatenate(near, axis=1)], axis=0)
    scores = mm(jnp.concatenate([w2s_ref[...], w2n_ref[...]], axis=1), both).T
    for g in range(4):
        for step, scores_ref in enumerate(scores_refs):

            @pl.when(lax.rem(place_ref[0] + step, 4) == g)
            def _():
                scores_ref[...] = scores[g * TGT : (g + 1) * TGT]

    head = mm_nt(classes, both)

    def pieces(side):
        for z in range(8):
            rows = []
            for f in range(16):
                tile = (z - 6 * f) % 8
                if tile < 6:
                    start = f * 96 + side * 48 + tile * 8
                    rows.append(grad[start : start + 8])
            rows.append(head[z * CLS_PAD : (z + 1) * CLS_PAD, side * 256 : (side + 1) * 256])
            yield z, jnp.concatenate(rows, axis=0)

    for side in range(2):

        @pl.when(place_ref[1] == side)
        def _():
            for z, piece in pieces(side):
                keep_ref[z] = piece
            for z, piece in pieces(1 - side):
                send_ref[z] = piece.astype(BF)


def layers(position, st, wt, targets, w2s_x, w2n_x):
    return pl.pallas_call(
        layers_kernel,
        out_shape=(
            jax.ShapeDtypeStruct((8, PIECE, 256), F32),
            jax.ShapeDtypeStruct((8, PIECE, 256), BF),
            *[jax.ShapeDtypeStruct((TGT, 153), F32)] * 4,
        ),
        in_specs=[pl.BlockSpec(memory_space=pltpu.SMEM)] + vmem(5),
        out_specs=tuple(vmem(6)),
        cost_estimate=pl.CostEstimate(flops=6_000_000_000, bytes_accessed=4_000_000, transcendentals=200_000),
        compiler_params=SMALL,
        name="layers",
    )(position, st, wt, targets, w2s_x, w2n_x)


def add_pair_kernel(keep_ref, came_ref, out_ref):
    for z in range(8):
        out_ref[z] = (keep_ref[z] + came_ref[z].astype(F32)).astype(BF)


def add_pair(keep, came):
    return pl.pallas_call(
        add_pair_kernel,
        out_shape=jax.ShapeDtypeStruct(came.shape, BF),
        in_specs=vmem(2),
        out_specs=vmem(1)[0],
        cost_estimate=pl.CostEstimate(flops=1_000_000, bytes_accessed=2_000_000, transcendentals=0),
        compiler_params=SMALL,
        name="add_pair",
    )(keep, came)


def sum_z_kernel(z_ref, in_ref, out_ref, total):
    total[...] = sum(in_ref[z].astype(F32) for z in range(8))
    absent = 3 - lax.div(z_ref[0], 2)
    for f in range(16):
        slot = (f // 4) * 3 + f % 4 - (f % 4 > absent).astype(jnp.int32)
        own = total[pl.ds(pl.multiple_of(slot * 8, 8), 8), :]
        out_ref[f] = jnp.concatenate([own, total[96 : 96 + CLS_PAD]], axis=0).astype(BF)


def sum_z(z, parts):
    return pl.pallas_call(
        sum_z_kernel,
        out_shape=jax.ShapeDtypeStruct((16, 8 + CLS_PAD, 256), BF),
        in_specs=[pl.BlockSpec(memory_space=pltpu.SMEM)] + vmem(1),
        out_specs=vmem(1)[0],
        scratch_shapes=[pltpu.VMEM((PIECE, 256), F32)],
        cost_estimate=pl.CostEstimate(flops=10_000_000, bytes_accessed=1_500_000, transcendentals=0),
        compiler_params=SMALL,
        name="sum_z",
    )(z, parts)


def sum_y_kernel(in_ref, out_ref):
    for x in range(4):
        total = sum(in_ref[4 * y + x].astype(F32) for y in range(4))
        out_ref[:, x * 256 : (x + 1) * 256] = total[: 8 + CLS_ROWS].astype(BF)


def sum_y(parts):
    return pl.pallas_call(
        sum_y_kernel,
        out_shape=jax.ShapeDtypeStruct((8 + CLS_ROWS, 1024), BF),
        in_specs=vmem(1),
        out_specs=vmem(1)[0],
        cost_estimate=pl.CostEstimate(flops=1_000_000, bytes_accessed=600_000, transcendentals=0),
        compiler_params=SMALL,
        name="sum_y",
    )(parts)


def place_kernel(x_ref, in_ref, score0, score1, score2, score3, logits_ref, self_ref, neigh_ref, head_self_ref, head_neigh_ref):
    logits_ref[...] = (score0[...] + score1[...] + score2[...] + score3[...]).astype(BF)
    for side, (first_ref, head_ref) in enumerate(((self_ref, head_self_ref), (neigh_ref, head_neigh_ref))):
        for tile in range(6):
            owner = lax.rem(tile + 6 * x_ref[0], 8)
            first_ref[tile * 8 : (tile + 1) * 8] = in_ref[2 * owner + side].astype(F32)[:8]
        for z in range(8):
            end = min((z + 1) * CLS_ROWS, 153)
            head_ref[z * CLS_ROWS : end] = in_ref[2 * z + side].astype(F32)[8 : 8 + end - z * CLS_ROWS]


def place(x, parts, scores):
    first = jax.ShapeDtypeStruct((48, 1024), F32)
    head = jax.ShapeDtypeStruct((153, 1024), F32)
    return pl.pallas_call(
        place_kernel,
        out_shape=(jax.ShapeDtypeStruct((TGT, 153), BF), first, first, head, head),
        in_specs=[pl.BlockSpec(memory_space=pltpu.SMEM)] + vmem(5),
        out_specs=tuple(vmem(5)),
        cost_estimate=pl.CostEstimate(flops=1_000_000, bytes_accessed=2_500_000, transcendentals=0),
        compiler_params=SMALL,
        name="place",
    )(x, parts, *scores)


def shifted(parts, axis):
    moves = [[(source, (source + step) % 4) for source in range(4)] for step in range(4)]
    return [parts[0]] + [lax.ppermute(parts[step], axis, moves[step]) for step in (1, 2, 3)]


def on_device(
    feature_table,
    node_ids,
    neigh_one,
    count_one,
    neigh_two,
    count_two,
    w_one_self,
    w_one_neigh,
    w_two_self,
    w_two_neigh,
    logit_grad,
):
    x, y, z, c = [lax.axis_index(axis).reshape(1) for axis in ("x", "y", "z", "c")]
    sent = pack(c, w_one_self, w_one_neigh, logit_grad[0], neigh_two.transpose(1, 0, 2), count_two)
    received = lax.all_to_all(sent, FEAT, 0, 0, tiled=True)
    gathered = gather(node_ids, neigh_one.transpose(1, 0, 2), count_one, feature_table)
    st = lax.all_to_all(gathered, FEAT, 0, 0, tiled=True)

    w2s_x = lax.dynamic_slice_in_dim(w_two_self.T, x[0] * 256, 256, 1)
    w2n_x = lax.dynamic_slice_in_dim(w_two_neigh.T, x[0] * 256, 256, 1)
    came = lax.ppermute(received, "c", [(0, 1), (1, 0)])
    wt, targets = turn_weights(jnp.concatenate([y, c]), received, came)
    position = jnp.concatenate([x, c])
    keep, send, *scores = layers(
        position, st.reshape(1536, 4 * SUB), wt, targets, w2s_x, w2n_x
    )
    scores = shifted(scores, "x")

    pair = add_pair(keep, lax.ppermute(send, "c", [(0, 1), (1, 0)]))
    pair, scores = lax.optimization_barrier((lax.all_to_all(pair, "z", 0, 0, tiled=True), scores))
    over_z = sum_z(z, pair)
    final = sum_y(lax.all_to_all(over_z, FEAT, 0, 0, tiled=True))
    final = lax.all_gather(final, REP, axis=0)
    logits, grad_self, grad_neigh, head_self, head_neigh = place(x, final, scores)
    return logits[None], grad_self, grad_neigh, head_self.T, head_neigh.T


def solution(mesh):
    fine = Mesh(np.asarray(mesh.devices).reshape(4, 4, 8, 2), ("y", "x", "z", "c"))
    return jax.shard_map(
        on_device,
        mesh=fine,
        in_specs=(
            P(FEAT, None),
            P(REP, None),
            P(REP, None, None),
            P(REP, None),
            P(REP, None, FEAT),
            P(REP, FEAT),
            P(FEAT, None),
            P(FEAT, None),
            P(),
            P(),
            P(REP, FEAT, None),
        ),
        out_specs=(P(REP, FEAT, None), P(FEAT, None), P(FEAT, None), P(), P()),
        check_vma=False,
    )
```

```python
import functools

import jax
import jax.numpy as jnp
import numpy as np
from jax import lax
from jax.experimental import pallas as pl
from jax.experimental.pallas import tpu as pltpu
from jax.sharding import Mesh, PartitionSpec as P

BF = jnp.bfloat16
F32 = jnp.float32
GELU_C = 0.7978845608028654
SMALL = pltpu.CompilerParams(vmem_limit_bytes=8 * 2**20)
FEAT = ("y", "x")
REP = ("z", "c")
SUB = 128
INP = 512
TGT = 64
CHUNK = 4096
LISTS = 160
CLS_ROWS = 20
CLS_PAD = 24
PIECE = 120


def mm(first, second):
    return jnp.dot(first, second, preferred_element_type=F32)


def mm_nt(first, second):
    return lax.dot_general(first, second, (((1,), (1,)), ((), ())), preferred_element_type=F32)


def vmem(count):
    return [pl.BlockSpec(memory_space=pltpu.VMEM)] * count


def gather_kernel(
    ids_hbm, neigh_hbm, count_hbm, table_hbm, out_hbm, ids_ref, neigh_ref, count_ref, table, turned, even, odd, held, arrived, sent
):
    cols, papers = table_hbm.shape
    fan = neigh_hbm.shape[0]
    share = -(-INP // (fan + 1))

    blocks = [pl.ds(start, CHUNK) for start in range(0, papers, CHUNK)]
    copies = [
        pltpu.make_async_copy(table_hbm.at[:, block], table.at[:, block], arrived.at[at])
        for at, block in enumerate(blocks)
    ]
    lists = [
        pltpu.make_async_copy(source, target, arrived.at[len(blocks) + at])
        for at, (source, target) in enumerate(((ids_hbm, ids_ref), (neigh_hbm, neigh_ref), (count_hbm, count_ref)))
    ]
    for copy in copies + lists:
        copy.start()
    for block, copy in zip(blocks, copies):
        copy.wait()
        turned[block, :cols] = table[:, block].T.astype(F32)
    for copy in lists:
        copy.wait()

    position = lax.broadcasted_iota(jnp.int32, (INP // 2, SUB), 0).astype(F32).astype(BF)
    one = jnp.ones((INP // 2, SUB), BF)
    zero = jnp.zeros((INP // 2, SUB), BF)

    def fetch(g, rows, first, last):
        for j in range(first, last):
            rows[pl.ds(j, 1), :] = turned[pl.ds(ids_ref[0, g * INP + j], 1), :]

    def sub_batch(g, rows, later, later_rows):
        nodes = pl.ds(pl.multiple_of(g * SUB, SUB), SUB)
        count = count_ref[:, nodes]
        halves = [zero, zero]
        for k in range(fan):
            fetch(later, later_rows, k * share, (k + 1) * share)
            near = jnp.where(k < count, neigh_ref[k, :, nodes], -1)
            for h in range(2):
                here = (near - h * (INP // 2)).astype(F32).astype(BF)
                halves[h] = halves[h] + jnp.where(position == here, one, zero)
        fetch(later, later_rows, fan * share, INP)
        picked = rows[...].astype(BF).T[:cols]
        summed = mm(picked[:, : INP // 2], halves[0]) + mm(picked[:, INP // 2 :], halves[1])
        agg = (summed / count.astype(F32)).astype(BF)
        own = picked[:, :SUB]
        lanes = pl.ds(pl.multiple_of((g % 4) * SUB, SUB), SUB)
        held[g // 4, :cols, lanes] = own
        held[g // 4, cols:, lanes] = agg

    def send(y, x):
        return pltpu.make_async_copy(held.at[y], out_hbm.at[4 * y + x], sent.at[4 * y + x])

    fetch(0, even, 0, INP)

    def pair(step, carry):
        sub_batch(2 * step, even, 2 * step + 1, odd)
        sub_batch(2 * step + 1, odd, jnp.minimum(2 * step + 2, 15), even)

        @pl.when(step % 2 == 1)
        def _():
            for x in range(4):
                send(step // 2, x).start()

        return carry

    lax.fori_loop(0, 8, pair, 0)
    for y in range(4):
        for x in range(4):
            send(y, x).wait()


def gather(node_ids, neigh_one, count_one, feature_table):
    cols, papers = feature_table.shape
    return pl.pallas_call(
        gather_kernel,
        out_shape=jax.ShapeDtypeStruct((16, 2 * cols, 4 * SUB), BF),
        in_specs=[pl.BlockSpec(memory_space=pl.ANY)] * 4,
        out_specs=pl.BlockSpec(memory_space=pl.ANY),
        scratch_shapes=[
            pltpu.SMEM(node_ids.shape, jnp.int32),
            pltpu.VMEM(neigh_one.shape, jnp.int32),
            pltpu.VMEM(count_one.shape, jnp.int32),
            pltpu.VMEM((cols, papers), BF),
            pltpu.VMEM((papers, 128), F32),
            pltpu.VMEM((INP, 128), F32),
            pltpu.VMEM((INP, 128), F32),
            pltpu.VMEM((4, 2 * cols, 4 * SUB), BF),
            pltpu.SemaphoreType.DMA((papers // CHUNK + 3,)),
            pltpu.SemaphoreType.DMA((16,)),
        ],
        compiler_params=pltpu.CompilerParams(vmem_limit_bytes=56 * 2**20),
        cost_estimate=pl.CostEstimate(flops=30_000_000_000, bytes_accessed=5_000_000, transcendentals=0),
        name="gather",
    )(node_ids, neigh_one, count_one, feature_table)


def pack_kernel(c_ref, w_self_ref, w_neigh_ref, up_ref, neigh_ref, count_ref, out_ref):
    near = [neigh_ref[k] for k in range(neigh_ref.shape[0])]
    lists = jnp.concatenate(near + [count_ref[...], jnp.zeros((6, TGT), jnp.int32)], axis=0).astype(F32)
    turned = jnp.concatenate([up_ref[...].astype(F32).T, jnp.zeros((7, TGT), F32), lists], axis=0)
    target = jnp.concatenate([turned[k * 48 : (k + 1) * 48] for k in range(4)], axis=1).astype(BF)
    for x in range(4):
        lanes = slice(x * 256, (x + 1) * 256)
        for y in range(4):
            out_ref[4 * y + x, 48:] = target
            for side, w_ref in enumerate((w_self_ref, w_neigh_ref)):

                @pl.when(c_ref[0] == side)
                def _():
                    out_ref[4 * y + x, :48] = w_ref[:, lanes]


def pack(c, w_self, w_neigh, upstream, neigh, count):
    return pl.pallas_call(
        pack_kernel,
        out_shape=jax.ShapeDtypeStruct((16, 96, 256), BF),
        in_specs=[pl.BlockSpec(memory_space=pltpu.SMEM)] + vmem(5),
        out_specs=vmem(1)[0],
        cost_estimate=pl.CostEstimate(flops=1_000_000, bytes_accessed=1_500_000, transcendentals=0),
        name="pack",
    )(c, w_self, w_neigh, upstream, neigh, count)


def turn_weights_kernel(place_ref, in_ref, came_ref, wt_ref, targets_ref):
    for side in range(2):

        @pl.when(place_ref[1] == side)
        def _():
            sides = (in_ref, came_ref) if side == 0 else (came_ref, in_ref)
            wt_ref[...] = jnp.concatenate([ref[f, :48] for f in range(16) for ref in sides], axis=0).T

    for g in range(4):
        targets_ref[g] = in_ref[4 * place_ref[0] + g, 48:]


def turn_weights(position, received, came):
    return pl.pallas_call(
        turn_weights_kernel,
        out_shape=(jax.ShapeDtypeStruct((256, 1536), BF), jax.ShapeDtypeStruct((4, 48, 256), BF)),
        in_specs=[pl.BlockSpec(memory_space=pltpu.SMEM)] + vmem(2),
        out_specs=tuple(vmem(2)),
        cost_estimate=pl.CostEstimate(flops=1_000_000, bytes_accessed=2_000_000, transcendentals=0),
        compiler_params=SMALL,
        name="turn_weights",
    )(position, received, came)


def layers_kernel(place_ref, st_ref, wt_ref, targets_ref, w2s_ref, w2n_ref, keep_ref, send_ref, *scores_refs):
    position = lax.broadcasted_iota(jnp.int32, (SUB, TGT), 0).astype(F32)
    classes, spreads, hidden_grads, counts = [], [], [], []
    for g in range(4):
        target = targets_ref[g].astype(F32)
        turned = jnp.concatenate([target[:, k * TGT : (k + 1) * TGT] for k in range(4)], axis=0)
        upstream = turned[:153].T.astype(BF)
        count = turned[LISTS + 25 : LISTS + 26]
        spread = jnp.zeros((SUB, TGT), F32)
        for k in range(25):
            near = jnp.where(k < count, turned[LISTS + k : LISTS + k + 1], -1.0)
            spread = spread + jnp.where(position == near, 1.0, 0.0)
        spread = spread.astype(BF)
        spreads.append(spread)
        own = mm(upstream, w2s_ref[...])
        near_grad = mm(upstream, w2n_ref[...]).T / count
        high = near_grad.astype(BF)
        low = (near_grad - high.astype(F32)).astype(BF)
        grad = mm_nt(high, spread) + mm_nt(low, spread)
        hidden_grads.append(grad + jnp.concatenate([own.T, jnp.zeros(own.T.shape, F32)], axis=1))
        classes.append(turned[:153])
        counts.append(count)
    classes = jnp.concatenate(classes, axis=1)
    blocks = []
    for z in range(8):
        block = classes[z * CLS_ROWS : min((z + 1) * CLS_ROWS, 153)]
        blocks += [block, jnp.zeros((CLS_PAD - block.shape[0], 4 * TGT), F32)]
    classes = jnp.concatenate(blocks, axis=0).astype(BF)

    pre = mm(wt_ref[...], st_ref[...])
    square = pre * pre
    bend = jnp.tanh(GELU_C * pre * (1.0 + 0.044715 * square))
    half = 0.5 * (1.0 + bend)
    hidden = (pre * half).astype(BF)
    slope = half + 0.5 * pre * (1.0 - bend * bend) * (GELU_C * (1.0 + 3.0 * 0.044715 * square))
    grad_pre = (jnp.concatenate(hidden_grads, axis=1) * slope).astype(BF)
    grad = mm_nt(st_ref[...], grad_pre)
    own, near = [], []
    for g in range(4):
        nodes = hidden[:, g * SUB : (g + 1) * SUB]
        own.append(nodes[:, :TGT])
        near.append((mm(nodes, spreads[g]) / counts[g]).astype(BF))
    both = jnp.concatenate([jnp.concatenate(own, axis=1), jnp.concatenate(near, axis=1)], axis=0)
    scores = mm(jnp.concatenate([w2s_ref[...], w2n_ref[...]], axis=1), both).T
    for g in range(4):
        for step, scores_ref in enumerate(scores_refs):

            @pl.when(lax.rem(place_ref[0] + step, 4) == g)
            def _():
                scores_ref[...] = scores[g * TGT : (g + 1) * TGT]

    head = mm_nt(classes, both)

    def pieces(side):
        for z in range(8):
            rows = []
            for f in range(16):
                tile = (z - 6 * f) % 8
                if tile < 6:
                    start = f * 96 + side * 48 + tile * 8
                    rows.append(grad[start : start + 8])
            rows.append(head[z * CLS_PAD : (z + 1) * CLS_PAD, side * 256 : (side + 1) * 256])
            yield z, jnp.concatenate(rows, axis=0)

    for side in range(2):

        @pl.when(place_ref[1] == side)
        def _():
            for z, piece in pieces(side):
                keep_ref[z] = piece
            for z, piece in pieces(1 - side):
                send_ref[z] = piece.astype(BF)


def layers(position, st, wt, targets, w2s_x, w2n_x):
    return pl.pallas_call(
        layers_kernel,
        out_shape=(
            jax.ShapeDtypeStruct((8, PIECE, 256), F32),
            jax.ShapeDtypeStruct((8, PIECE, 256), BF),
            *[jax.ShapeDtypeStruct((TGT, 153), F32)] * 4,
        ),
        in_specs=[pl.BlockSpec(memory_space=pltpu.SMEM)] + vmem(5),
        out_specs=tuple(vmem(6)),
        cost_estimate=pl.CostEstimate(flops=6_000_000_000, bytes_accessed=4_000_000, transcendentals=200_000),
        compiler_params=SMALL,
        name="layers",
    )(position, st, wt, targets, w2s_x, w2n_x)


def add_pair_kernel(keep_ref, came_ref, out_ref):
    for z in range(8):
        out_ref[z] = (keep_ref[z] + came_ref[z].astype(F32)).astype(BF)


def add_pair(keep, came):
    return pl.pallas_call(
        add_pair_kernel,
        out_shape=jax.ShapeDtypeStruct(came.shape, BF),
        in_specs=vmem(2),
        out_specs=vmem(1)[0],
        cost_estimate=pl.CostEstimate(flops=1_000_000, bytes_accessed=2_000_000, transcendentals=0),
        compiler_params=SMALL,
        name="add_pair",
    )(keep, came)


def sum_z_kernel(z_ref, in_ref, out_ref, total):
    total[...] = sum(in_ref[z].astype(F32) for z in range(8))
    absent = 3 - lax.div(z_ref[0], 2)
    for f in range(16):
        slot = (f // 4) * 3 + f % 4 - (f % 4 > absent).astype(jnp.int32)
        own = total[pl.ds(pl.multiple_of(slot * 8, 8), 8), :]
        out_ref[f] = jnp.concatenate([own, total[96 : 96 + CLS_PAD]], axis=0).astype(BF)


def sum_z(z, parts):
    return pl.pallas_call(
        sum_z_kernel,
        out_shape=jax.ShapeDtypeStruct((16, 8 + CLS_PAD, 256), BF),
        in_specs=[pl.BlockSpec(memory_space=pltpu.SMEM)] + vmem(1),
        out_specs=vmem(1)[0],
        scratch_shapes=[pltpu.VMEM((PIECE, 256), F32)],
        cost_estimate=pl.CostEstimate(flops=10_000_000, bytes_accessed=1_500_000, transcendentals=0),
        compiler_params=SMALL,
        name="sum_z",
    )(z, parts)


def sum_y_kernel(in_ref, out_ref):
    for x in range(4):
        total = sum(in_ref[4 * y + x].astype(F32) for y in range(4))
        out_ref[:, x * 256 : (x + 1) * 256] = total[: 8 + CLS_ROWS].astype(BF)


def sum_y(parts):
    return pl.pallas_call(
        sum_y_kernel,
        out_shape=jax.ShapeDtypeStruct((8 + CLS_ROWS, 1024), BF),
        in_specs=vmem(1),
        out_specs=vmem(1)[0],
        cost_estimate=pl.CostEstimate(flops=1_000_000, bytes_accessed=600_000, transcendentals=0),
        compiler_params=SMALL,
        name="sum_y",
    )(parts)


def place_kernel(x_ref, in_ref, score0, score1, score2, score3, logits_ref, self_ref, neigh_ref, head_self_ref, head_neigh_ref):
    logits_ref[...] = (score0[...] + score1[...] + score2[...] + score3[...]).astype(BF)
    for side, (first_ref, head_ref) in enumerate(((self_ref, head_self_ref), (neigh_ref, head_neigh_ref))):
        for tile in range(6):
            owner = lax.rem(tile + 6 * x_ref[0], 8)
            first_ref[tile * 8 : (tile + 1) * 8] = in_ref[2 * owner + side].astype(F32)[:8]
        for z in range(8):
            end = min((z + 1) * CLS_ROWS, 153)
            head_ref[z * CLS_ROWS : end] = in_ref[2 * z + side].astype(F32)[8 : 8 + end - z * CLS_ROWS]


def place(x, parts, scores):
    first = jax.ShapeDtypeStruct((48, 1024), F32)
    head = jax.ShapeDtypeStruct((153, 1024), F32)
    return pl.pallas_call(
        place_kernel,
        out_shape=(jax.ShapeDtypeStruct((TGT, 153), BF), first, first, head, head),
        in_specs=[pl.BlockSpec(memory_space=pltpu.SMEM)] + vmem(5),
        out_specs=tuple(vmem(5)),
        cost_estimate=pl.CostEstimate(flops=1_000_000, bytes_accessed=2_500_000, transcendentals=0),
        compiler_params=SMALL,
        name="place",
    )(x, parts, *scores)


def shifted(parts, axis):
    moves = [[(source, (source + step) % 4) for source in range(4)] for step in range(4)]
    return [parts[0]] + [lax.ppermute(parts[step], axis, moves[step]) for step in (1, 2, 3)]


def on_device(
    feature_table,
    node_ids,
    neigh_one,
    count_one,
    neigh_two,
    count_two,
    w_one_self,
    w_one_neigh,
    w_two_self,
    w_two_neigh,
    logit_grad,
):
    x, y, z, c = [lax.axis_index(axis).reshape(1) for axis in ("x", "y", "z", "c")]
    sent = pack(c, w_one_self, w_one_neigh, logit_grad[0], neigh_two.transpose(1, 0, 2), count_two)
    received = lax.all_to_all(sent, FEAT, 0, 0, tiled=True)
    gathered = gather(node_ids, neigh_one.transpose(1, 0, 2), count_one, feature_table)
    st = lax.all_to_all(gathered, FEAT, 0, 0, tiled=True)

    w2s_x = lax.dynamic_slice_in_dim(w_two_self.T, x[0] * 256, 256, 1)
    w2n_x = lax.dynamic_slice_in_dim(w_two_neigh.T, x[0] * 256, 256, 1)
    came = lax.ppermute(received, "c", [(0, 1), (1, 0)])
    wt, targets = turn_weights(jnp.concatenate([y, c]), received, came)
    position = jnp.concatenate([x, c])
    keep, send, *scores = layers(
        position, st.reshape(1536, 4 * SUB), wt, targets, w2s_x, w2n_x
    )
    scores = shifted(scores, "x")

    pair = add_pair(keep, lax.ppermute(send, "c", [(0, 1), (1, 0)]))
    pair, scores = lax.optimization_barrier((lax.all_to_all(pair, "z", 0, 0, tiled=True), scores))
    over_z = sum_z(z, pair)
    final = sum_y(lax.all_to_all(over_z, FEAT, 0, 0, tiled=True))
    final = lax.all_gather(final, REP, axis=0)
    logits, grad_self, grad_neigh, head_self, head_neigh = place(x, final, scores)
    return logits[None], grad_self, grad_neigh, head_self.T, head_neigh.T


def solution(mesh):
    fine = Mesh(np.asarray(mesh.devices).reshape(4, 4, 8, 2), ("y", "x", "z", "c"))
    return jax.shard_map(
        on_device,
        mesh=fine,
        in_specs=(
            P(FEAT, None),
            P(REP, None),
            P(REP, None, None),
            P(REP, None),
            P(REP, None, FEAT),
            P(REP, FEAT),
            P(FEAT, None),
            P(FEAT, None),
            P(),
            P(),
            P(REP, FEAT, None),
        ),
        out_specs=(P(REP, FEAT, None), P(FEAT, None), P(FEAT, None), P(), P()),
        check_vma=False,
    )
```

```python
import functools

import jax
import jax.numpy as jnp
import numpy as np
from jax import lax
from jax.experimental import pallas as pl
from jax.experimental.pallas import tpu as pltpu
from jax.sharding import Mesh, PartitionSpec as P

BF = jnp.bfloat16
F32 = jnp.float32
GELU_C = 0.7978845608028654
SMALL = pltpu.CompilerParams(vmem_limit_bytes=8 * 2**20)
FEAT = ("y", "x")
REP = ("z", "c")
SUB = 128
INP = 512
TGT = 64
CHUNK = 4096
LISTS = 160
CLS_ROWS = 20
CLS_PAD = 24
PIECE = 120


def mm(first, second):
    return jnp.dot(first, second, preferred_element_type=F32)


def mm_nt(first, second):
    return lax.dot_general(first, second, (((1,), (1,)), ((), ())), preferred_element_type=F32)


def vmem(count):
    return [pl.BlockSpec(memory_space=pltpu.VMEM)] * count


def gather_kernel(
    ids_hbm, neigh_hbm, count_hbm, table_hbm, out_hbm, ids_ref, neigh_ref, count_ref, table, turned, even, odd, held, arrived, sent
):
    cols, papers = table_hbm.shape
    fan = neigh_hbm.shape[0]
    share = -(-INP // (fan + 1))

    blocks = [pl.ds(start, CHUNK) for start in range(0, papers, CHUNK)]
    copies = [
        pltpu.make_async_copy(table_hbm.at[:, block], table.at[:, block], arrived.at[at])
        for at, block in enumerate(blocks)
    ]
    lists = [
        pltpu.make_async_copy(source, target, arrived.at[len(blocks) + at])
        for at, (source, target) in enumerate(((ids_hbm, ids_ref), (neigh_hbm, neigh_ref), (count_hbm, count_ref)))
    ]
    for copy in copies + lists:
        copy.start()
    for block, copy in zip(blocks, copies):
        copy.wait()
        turned[block, :cols] = table[:, block].T.astype(F32)
    for copy in lists:
        copy.wait()

    position = lax.broadcasted_iota(jnp.int32, (INP // 2, SUB), 0).astype(F32).astype(BF)
    one = jnp.ones((INP // 2, SUB), BF)
    zero = jnp.zeros((INP // 2, SUB), BF)

    def fetch(g, rows, first, last):
        for j in range(first, last):
            rows[pl.ds(j, 1), :] = turned[pl.ds(ids_ref[0, g * INP + j], 1), :]

    def sub_batch(g, rows, later, later_rows):
        nodes = pl.ds(pl.multiple_of(g * SUB, SUB), SUB)
        count = count_ref[:, nodes]
        halves = [zero, zero]
        for k in range(fan):
            fetch(later, later_rows, k * share, (k + 1) * share)
            near = jnp.where(k < count, neigh_ref[k, :, nodes], -1)
            for h in range(2):
                here = (near - h * (INP // 2)).astype(F32).astype(BF)
                halves[h] = halves[h] + jnp.where(position == here, one, zero)
        fetch(later, later_rows, fan * share, INP)
        picked = rows[...].astype(BF).T[:cols]
        summed = mm(picked[:, : INP // 2], halves[0]) + mm(picked[:, INP // 2 :], halves[1])
        agg = (summed / count.astype(F32)).astype(BF)
        own = picked[:, :SUB]
        lanes = pl.ds(pl.multiple_of((g % 4) * SUB, SUB), SUB)
        held[g // 4, :cols, lanes] = own
        held[g // 4, cols:, lanes] = agg

    def send(y, x):
        return pltpu.make_async_copy(held.at[y], out_hbm.at[4 * y + x], sent.at[4 * y + x])

    fetch(0, even, 0, INP)

    def pair(step, carry):
        sub_batch(2 * step, even, 2 * step + 1, odd)
        sub_batch(2 * step + 1, odd, jnp.minimum(2 * step + 2, 15), even)

        @pl.when(step % 2 == 1)
        def _():
            for x in range(4):
                send(step // 2, x).start()

        return carry

    lax.fori_loop(0, 8, pair, 0)
    for y in range(4):
        for x in range(4):
            send(y, x).wait()


def gather(node_ids, neigh_one, count_one, feature_table):
    cols, papers = feature_table.shape
    return pl.pallas_call(
        gather_kernel,
        out_shape=jax.ShapeDtypeStruct((16, 2 * cols, 4 * SUB), BF),
        in_specs=[pl.BlockSpec(memory_space=pl.ANY)] * 4,
        out_specs=pl.BlockSpec(memory_space=pl.ANY),
        scratch_shapes=[
            pltpu.SMEM(node_ids.shape, jnp.int32),
            pltpu.VMEM(neigh_one.shape, jnp.int32),
            pltpu.VMEM(count_one.shape, jnp.int32),
            pltpu.VMEM((cols, papers), BF),
            pltpu.VMEM((papers, 128), F32),
            pltpu.VMEM((INP, 128), F32),
            pltpu.VMEM((INP, 128), F32),
            pltpu.VMEM((4, 2 * cols, 4 * SUB), BF),
            pltpu.SemaphoreType.DMA((papers // CHUNK + 3,)),
            pltpu.SemaphoreType.DMA((16,)),
        ],
        compiler_params=pltpu.CompilerParams(vmem_limit_bytes=56 * 2**20),
        cost_estimate=pl.CostEstimate(flops=30_000_000_000, bytes_accessed=5_000_000, transcendentals=0),
        name="gather",
    )(node_ids, neigh_one, count_one, feature_table)


def pack_kernel(c_ref, w_self_hbm, w_neigh_hbm, up_hbm, neigh_hbm, count_hbm, out_ref, w_ref, up_ref, neigh_ref, count_ref, arrived):
    copies = [
        pltpu.make_async_copy(source, target, arrived.at[at])
        for at, (source, target) in enumerate(((up_hbm, up_ref), (neigh_hbm, neigh_ref), (count_hbm, count_ref)))
    ]
    for copy in copies:
        copy.start()
    for side, w_hbm in enumerate((w_self_hbm, w_neigh_hbm)):

        @pl.when(c_ref[0] == side)
        def _():
            copy = pltpu.make_async_copy(w_hbm, w_ref, arrived.at[3 + side])
            copy.start()
            copy.wait()

    for copy in copies:
        copy.wait()
    near = [neigh_ref[k] for k in range(neigh_ref.shape[0])]
    lists = jnp.concatenate(near + [count_ref[...], jnp.zeros((6, TGT), jnp.int32)], axis=0).astype(F32)
    turned = jnp.concatenate([up_ref[...].astype(F32).T, jnp.zeros((7, TGT), F32), lists], axis=0)
    target = jnp.concatenate([turned[k * 48 : (k + 1) * 48] for k in range(4)], axis=1).astype(BF)
    for x in range(4):
        for y in range(4):
            out_ref[4 * y + x, :48] = w_ref[:, x * 256 : (x + 1) * 256]
            out_ref[4 * y + x, 48:] = target


def pack(c, w_self, w_neigh, upstream, neigh, count):
    return pl.pallas_call(
        pack_kernel,
        out_shape=jax.ShapeDtypeStruct((16, 96, 256), BF),
        in_specs=[pl.BlockSpec(memory_space=pltpu.SMEM)] + [pl.BlockSpec(memory_space=pl.ANY)] * 5,
        out_specs=vmem(1)[0],
        scratch_shapes=[
            pltpu.VMEM(w_self.shape, BF),
            pltpu.VMEM(upstream.shape, BF),
            pltpu.VMEM(neigh.shape, jnp.int32),
            pltpu.VMEM(count.shape, jnp.int32),
            pltpu.SemaphoreType.DMA((5,)),
        ],
        compiler_params=pltpu.CompilerParams(vmem_limit_bytes=56 * 2**20),
        cost_estimate=pl.CostEstimate(flops=1_000_000, bytes_accessed=1_500_000, transcendentals=0),
        name="pack",
    )(c, w_self, w_neigh, upstream, neigh, count)


def turn_weights_kernel(place_ref, in_ref, came_ref, wt_ref, targets_ref):
    for side in range(2):

        @pl.when(place_ref[1] == side)
        def _():
            sides = (in_ref, came_ref) if side == 0 else (came_ref, in_ref)
            wt_ref[...] = jnp.concatenate([ref[f, :48] for f in range(16) for ref in sides], axis=0).T

    for g in range(4):
        targets_ref[g] = in_ref[4 * place_ref[0] + g, 48:]


def turn_weights(position, received, came):
    return pl.pallas_call(
        turn_weights_kernel,
        out_shape=(jax.ShapeDtypeStruct((256, 1536), BF), jax.ShapeDtypeStruct((4, 48, 256), BF)),
        in_specs=[pl.BlockSpec(memory_space=pltpu.SMEM)] + vmem(2),
        out_specs=tuple(vmem(2)),
        cost_estimate=pl.CostEstimate(flops=1_000_000, bytes_accessed=2_000_000, transcendentals=0),
        compiler_params=SMALL,
        name="turn_weights",
    )(position, received, came)


def layers_kernel(place_ref, st_ref, wt_ref, targets_ref, w2s_ref, w2n_ref, keep_ref, send_ref, *scores_refs):
    position = lax.broadcasted_iota(jnp.int32, (SUB, TGT), 0).astype(F32)
    classes, spreads, hidden_grads, counts = [], [], [], []
    for g in range(4):
        target = targets_ref[g].astype(F32)
        turned = jnp.concatenate([target[:, k * TGT : (k + 1) * TGT] for k in range(4)], axis=0)
        upstream = turned[:153].T.astype(BF)
        count = turned[LISTS + 25 : LISTS + 26]
        spread = jnp.zeros((SUB, TGT), F32)
        for k in range(25):
            near = jnp.where(k < count, turned[LISTS + k : LISTS + k + 1], -1.0)
            spread = spread + jnp.where(position == near, 1.0, 0.0)
        spread = spread.astype(BF)
        spreads.append(spread)
        own = mm(upstream, w2s_ref[...])
        near_grad = mm(upstream, w2n_ref[...]).T / count
        high = near_grad.astype(BF)
        low = (near_grad - high.astype(F32)).astype(BF)
        grad = mm_nt(high, spread) + mm_nt(low, spread)
        hidden_grads.append(grad + jnp.concatenate([own.T, jnp.zeros(own.T.shape, F32)], axis=1))
        classes.append(turned[:153])
        counts.append(count)
    classes = jnp.concatenate(classes, axis=1)
    blocks = []
    for z in range(8):
        block = classes[z * CLS_ROWS : min((z + 1) * CLS_ROWS, 153)]
        blocks += [block, jnp.zeros((CLS_PAD - block.shape[0], 4 * TGT), F32)]
    classes = jnp.concatenate(blocks, axis=0).astype(BF)

    pre = mm(wt_ref[...], st_ref[...])
    square = pre * pre
    bend = jnp.tanh(GELU_C * pre * (1.0 + 0.044715 * square))
    half = 0.5 * (1.0 + bend)
    hidden = (pre * half).astype(BF)
    slope = half + 0.5 * pre * (1.0 - bend * bend) * (GELU_C * (1.0 + 3.0 * 0.044715 * square))
    grad_pre = (jnp.concatenate(hidden_grads, axis=1) * slope).astype(BF)
    grad = mm_nt(st_ref[...], grad_pre)
    own, near = [], []
    for g in range(4):
        nodes = hidden[:, g * SUB : (g + 1) * SUB]
        own.append(nodes[:, :TGT])
        near.append((mm(nodes, spreads[g]) / counts[g]).astype(BF))
    both = jnp.concatenate([jnp.concatenate(own, axis=1), jnp.concatenate(near, axis=1)], axis=0)
    scores = mm(jnp.concatenate([w2s_ref[...], w2n_ref[...]], axis=1), both).T
    for g in range(4):
        for step, scores_ref in enumerate(scores_refs):

            @pl.when(lax.rem(place_ref[0] + step, 4) == g)
            def _():
                scores_ref[...] = scores[g * TGT : (g + 1) * TGT]

    head = mm_nt(classes, both)

    def pieces(side):
        for z in range(8):
            rows = []
            for f in range(16):
                tile = (z - 6 * f) % 8
                if tile < 6:
                    start = f * 96 + side * 48 + tile * 8
                    rows.append(grad[start : start + 8])
            rows.append(head[z * CLS_PAD : (z + 1) * CLS_PAD, side * 256 : (side + 1) * 256])
            yield z, jnp.concatenate(rows, axis=0)

    for side in range(2):

        @pl.when(place_ref[1] == side)
        def _():
            for z, piece in pieces(side):
                keep_ref[z] = piece
            for z, piece in pieces(1 - side):
                send_ref[z] = piece.astype(BF)


def layers(position, st, wt, targets, w2s_x, w2n_x):
    return pl.pallas_call(
        layers_kernel,
        out_shape=(
            jax.ShapeDtypeStruct((8, PIECE, 256), F32),
            jax.ShapeDtypeStruct((8, PIECE, 256), BF),
            *[jax.ShapeDtypeStruct((TGT, 153), F32)] * 4,
        ),
        in_specs=[pl.BlockSpec(memory_space=pltpu.SMEM)] + vmem(5),
        out_specs=tuple(vmem(6)),
        cost_estimate=pl.CostEstimate(flops=6_000_000_000, bytes_accessed=4_000_000, transcendentals=200_000),
        compiler_params=SMALL,
        name="layers",
    )(position, st, wt, targets, w2s_x, w2n_x)


def add_pair_kernel(keep_ref, came_ref, out_ref):
    for z in range(8):
        out_ref[z] = (keep_ref[z] + came_ref[z].astype(F32)).astype(BF)


def add_pair(keep, came):
    return pl.pallas_call(
        add_pair_kernel,
        out_shape=jax.ShapeDtypeStruct(came.shape, BF),
        in_specs=vmem(2),
        out_specs=vmem(1)[0],
        cost_estimate=pl.CostEstimate(flops=1_000_000, bytes_accessed=2_000_000, transcendentals=0),
        compiler_params=SMALL,
        name="add_pair",
    )(keep, came)


def sum_z_kernel(z_ref, in_ref, out_ref, total):
    total[...] = sum(in_ref[z].astype(F32) for z in range(8))
    absent = 3 - lax.div(z_ref[0], 2)
    for f in range(16):
        slot = (f // 4) * 3 + f % 4 - (f % 4 > absent).astype(jnp.int32)
        own = total[pl.ds(pl.multiple_of(slot * 8, 8), 8), :]
        out_ref[f] = jnp.concatenate([own, total[96 : 96 + CLS_PAD]], axis=0).astype(BF)


def sum_z(z, parts):
    return pl.pallas_call(
        sum_z_kernel,
        out_shape=jax.ShapeDtypeStruct((16, 8 + CLS_PAD, 256), BF),
        in_specs=[pl.BlockSpec(memory_space=pltpu.SMEM)] + vmem(1),
        out_specs=vmem(1)[0],
        scratch_shapes=[pltpu.VMEM((PIECE, 256), F32)],
        cost_estimate=pl.CostEstimate(flops=10_000_000, bytes_accessed=1_500_000, transcendentals=0),
        compiler_params=SMALL,
        name="sum_z",
    )(z, parts)


def sum_y_kernel(in_ref, out_ref):
    parts = [sum(in_ref[4 * y + x].astype(F32) for y in range(4))[: 8 + CLS_ROWS] for x in range(4)]
    halves = [jnp.concatenate(parts[:2], axis=1), jnp.concatenate(parts[2:], axis=1)]
    out_ref[...] = jnp.concatenate(halves, axis=0).astype(BF)


def sum_y(parts):
    return pl.pallas_call(
        sum_y_kernel,
        out_shape=jax.ShapeDtypeStruct((2 * (8 + CLS_ROWS), 512), BF),
        in_specs=vmem(1),
        out_specs=vmem(1)[0],
        cost_estimate=pl.CostEstimate(flops=1_000_000, bytes_accessed=600_000, transcendentals=0),
        compiler_params=SMALL,
        name="sum_y",
    )(parts)


def place_kernel(x_ref, in_ref, score0, score1, score2, score3, logits_ref, self_ref, neigh_ref, head_self_ref, head_neigh_ref):
    logits_ref[...] = (score0[...] + score1[...] + score2[...] + score3[...]).astype(BF)
    for side, (first_ref, head_ref) in enumerate(((self_ref, head_self_ref), (neigh_ref, head_neigh_ref))):
        rows = 8 + CLS_ROWS
        for tile in range(6):
            owner = lax.rem(tile + 6 * x_ref[0], 8)
            piece = in_ref[2 * owner + side].astype(F32)
            for half in range(2):
                first_ref[tile * 8 : (tile + 1) * 8, half * 512 : (half + 1) * 512] = piece[half * rows : half * rows + 8]
        for z in range(8):
            end = min((z + 1) * CLS_ROWS, 153)
            piece = in_ref[2 * z + side].astype(F32)
            for half in range(2):
                start = half * rows + 8
                head_ref[z * CLS_ROWS : end, half * 512 : (half + 1) * 512] = piece[start : start + end - z * CLS_ROWS]


def place(x, parts, scores):
    first = jax.ShapeDtypeStruct((48, 1024), F32)
    head = jax.ShapeDtypeStruct((153, 1024), F32)
    return pl.pallas_call(
        place_kernel,
        out_shape=(jax.ShapeDtypeStruct((TGT, 153), BF), first, first, head, head),
        in_specs=[pl.BlockSpec(memory_space=pltpu.SMEM)] + vmem(5),
        out_specs=tuple(vmem(5)),
        cost_estimate=pl.CostEstimate(flops=1_000_000, bytes_accessed=2_500_000, transcendentals=0),
        compiler_params=SMALL,
        name="place",
    )(x, parts, *scores)


def shifted(parts, axis):
    moves = [[(source, (source + step) % 4) for source in range(4)] for step in range(4)]
    return [parts[0]] + [lax.ppermute(parts[step], axis, moves[step]) for step in (1, 2, 3)]


def on_device(
    feature_table,
    node_ids,
    neigh_one,
    count_one,
    neigh_two,
    count_two,
    w_one_self,
    w_one_neigh,
    w_two_self,
    w_two_neigh,
    logit_grad,
):
    x, y, z, c = [lax.axis_index(axis).reshape(1) for axis in ("x", "y", "z", "c")]
    sent = pack(c, w_one_self, w_one_neigh, logit_grad[0], neigh_two.transpose(1, 0, 2), count_two)
    received = lax.all_to_all(sent, FEAT, 0, 0, tiled=True)
    gathered = gather(node_ids, neigh_one.transpose(1, 0, 2), count_one, feature_table)
    st = lax.all_to_all(gathered, FEAT, 0, 0, tiled=True)

    w2s_x = lax.dynamic_slice_in_dim(w_two_self.T, x[0] * 256, 256, 1)
    w2n_x = lax.dynamic_slice_in_dim(w_two_neigh.T, x[0] * 256, 256, 1)
    came = lax.ppermute(received, "c", [(0, 1), (1, 0)])
    wt, targets = turn_weights(jnp.concatenate([y, c]), received, came)
    position = jnp.concatenate([x, c])
    keep, send, *scores = layers(
        position, st.reshape(1536, 4 * SUB), wt, targets, w2s_x, w2n_x
    )
    scores = shifted(scores, "x")

    pair = add_pair(keep, lax.ppermute(send, "c", [(0, 1), (1, 0)]))
    pair, scores = lax.optimization_barrier((lax.all_to_all(pair, "z", 0, 0, tiled=True), scores))
    over_z = sum_z(z, pair)
    final = sum_y(lax.all_to_all(over_z, FEAT, 0, 0, tiled=True))
    final = lax.all_gather(final, REP, axis=0)
    logits, grad_self, grad_neigh, head_self, head_neigh = place(x, final, scores)
    return logits[None], grad_self, grad_neigh, head_self.T, head_neigh.T


def solution(mesh):
    fine = Mesh(np.asarray(mesh.devices).reshape(4, 4, 8, 2), ("y", "x", "z", "c"))
    return jax.shard_map(
        on_device,
        mesh=fine,
        in_specs=(
            P(FEAT, None),
            P(REP, None),
            P(REP, None, None),
            P(REP, None),
            P(REP, None, FEAT),
            P(REP, FEAT),
            P(FEAT, None),
            P(FEAT, None),
            P(),
            P(),
            P(REP, FEAT, None),
        ),
        out_specs=(P(REP, FEAT, None), P(FEAT, None), P(FEAT, None), P(), P()),
        check_vma=False,
    )
```
